32 devices in a mesh: sub: 8 (over z, y), grp: 4 (over x, core).
Axes of the slice: x: 2, y: 2, z: 4, core: 2. Of those that a mesh axis runs over, the one named last changes fastest.
Arguments:
- deflation: bfloat16 [512, 32, 4, 128], P(None, 'sub', 'grp'), may hold values from -0.045643546 to 0.045643546
- shift_field: float32 [32, 4, 128], P('sub', 'grp'), may hold values from 0.5 to 8
- counts: int32 [8], P('sub'), may hold values from 128 to 512, as said below
- right_sides: float32 [4096, 256], P(('sub', 'grp')), may hold values from -6 to 6
Outputs:
- coarse_solution: float32 [4096, 256], P(('sub', 'grp'))
The draws below stay inside these ranges and needn't reach their ends.
Inputs may be any that keep to these rules, and one draw needn't show every extreme that they name: `counts`: live deflation vectors of each subdomain; some subdomain has 512 and some 512 // 4.
All inputs are finite; a program needn't handle non-finite values.
Results may differ from the reference program's by a relative error of at most 0.0014.
Values may be sent and summed in bfloat16 or wider, within the bound.
A program may use at most 64 MiB of HBM per device.

```python
import math
import jax
import jax.numpy as jnp
from jax import lax

KMAX = 512
CZ = 4
CX = 128
NRHS = 256
SWEEPS = 6
SUBS = 8
BLK = 128
NZ = 32
NY = 4
N_GRP = 4


def draw_deflation(key, part):
    key_common = jax.random.fold_in(key, 11)
    key_noise = jax.random.fold_in(key, 12)
    shape = (KMAX, NZ, NY, CX)
    common = 0.7 * jax.random.normal(key_common, (KMAX, 1, 1, 1), jnp.float32)
    noise = jax.random.normal(key_noise, shape, jnp.float32)
    values = jnp.clip(common + noise, -8.0, 8.0) / jnp.sqrt(15.0 * CZ * NY * CX)
    return values.astype(jnp.bfloat16)


def draw_counts(key, part):
    key_values = jax.random.fold_in(key, 21)
    key_high = jax.random.fold_in(key, 22)
    key_low = jax.random.fold_in(key, 23)
    values = jax.random.randint(key_values, (SUBS,), KMAX // 4, KMAX + 1, jnp.int32)
    high_index = jax.random.randint(key_high, (), 0, SUBS, jnp.int32)
    step_over = jax.random.randint(key_low, (), 1, SUBS, jnp.int32)
    low_index = (high_index + step_over) % SUBS
    values = values.at[high_index].set(KMAX)
    values = values.at[low_index].set(KMAX // 4)
    return values


def level_of(stream_key, dims, cuts, smallest, top_value):
    def one(axis_at, parts):
        draws = jax.random.uniform(jax.random.fold_in(jax.random.fold_in(stream_key, 6), axis_at), (parts,), jnp.float32, smallest / len(cuts), top_value / len(cuts))
        return jnp.repeat(jnp.exp(draws), dims[axis_at] // parts).reshape((-1,) + (1,) * (len(dims) - axis_at - 1))

    level = one(*cuts[0])
    for cut in cuts[1:]:
        level = level * one(*cut)
    return level


def bell_draw(key, extent, scale, reach, pieces=(), held_as=jnp.bfloat16):
    gain = level_of(key, extent, pieces, -0.22, 0.18) if pieces else 1.0
    values = jax.random.normal(key, extent, jnp.float32) * scale * gain
    return jnp.minimum(jnp.maximum(values, -reach), reach).astype(held_as)


def setup_inputs(seed: int = 0) -> dict:
    arg_keys = jax.random.split(jax.random.key(seed), 5)
    deflation = draw_deflation(jax.random.fold_in(arg_keys[4], 71), 0)
    shift_field = jnp.clip(jnp.exp(math.log(8.0) - 2.7725887 * jax.random.uniform(arg_keys[1], (NZ, NY, CX), jnp.float32) ** level_of(arg_keys[1], (NZ, NY, CX), ((0, 8), (1, 4)), -0.2, 0.2)), 0.5, 8.0)
    counts = draw_counts(jax.random.fold_in(arg_keys[4], 71), 0)
    right_sides = bell_draw(arg_keys[3], (SUBS * KMAX, NRHS), 1.0, 6.0, ((0, 32),), jnp.float32)
    return dict(deflation=deflation, shift_field=shift_field, counts=counts, right_sides=right_sides)


damping = 0.7

def smooth_last(values):
    width_x = values.shape[-1]
    positions = lax.iota(jnp.int32, width_x)
    left_side = jnp.where(positions >= 1, jnp.roll(values, 1, axis=-1), 0.0)
    right_side = jnp.where(positions < width_x - 1, jnp.roll(values, -1, axis=-1), 0.0)
    return values + 0.5 * (left_side + right_side)

def smooth_valid(values, which_axis):
    length = values.shape[which_axis]
    center = lax.slice_in_dim(values, 1, length - 1, axis=which_axis)
    lower = lax.slice_in_dim(values, 0, length - 2, axis=which_axis)
    upper = lax.slice_in_dim(values, 2, length, axis=which_axis)
    return center + 0.5 * (lower + upper)

def pad_axis(values, which_axis):
    widths = [(0, 0)] * values.ndim
    widths[which_axis] = (1, 1)
    return jnp.pad(values, widths)

def contract(left_part, right_part):
    return lax.dot_general(left_part.astype(jnp.float32), right_part.astype(jnp.float32), (((1,), (1,)), ((), ())), preferred_element_type=jnp.float32)

def reference(deflation, shift_field, counts, right_sides):
    slot_ids = lax.iota(jnp.int32, KMAX)

    def neighbour_plane(other, plane):
        valid = (other >= 0) & (other < SUBS)
        safe = jnp.clip(other, 0, SUBS - 1)
        plane_index = jnp.clip(plane, 0, NZ - 1).astype(jnp.int32)
        values = lax.dynamic_slice_in_dim(deflation, plane_index, 1, 1)[:, 0]
        live_other = (slot_ids < counts[safe]) & valid
        values = jnp.where(live_other[:, None, None], values, jnp.zeros((), deflation.dtype))
        along = smooth_valid(pad_axis(smooth_last(values.astype(jnp.float32)), 1), 1)
        return along.astype(jnp.bfloat16).reshape(KMAX, -1)

    def slab_rows(slab):
        begin = (slab * CZ).astype(jnp.int32)
        values = lax.dynamic_slice_in_dim(deflation, begin, CZ, 1)
        live_slots = slot_ids < counts[slab]
        masked = jnp.where(live_slots[:, None, None, None], values, jnp.zeros((), deflation.dtype))
        shift_slab = lax.dynamic_slice_in_dim(shift_field, begin, CZ, 0)
        own_field = masked.astype(jnp.float32)
        along_x = smooth_last(own_field)
        along_y = smooth_valid(pad_axis(along_x, 2), 2)
        along_z = smooth_valid(pad_axis(along_y, 1), 1)
        images = ((16.0 + shift_slab) * own_field - 2.0 * along_z).astype(jnp.bfloat16)
        above_plane = neighbour_plane(slab + 1, (slab + 1) * CZ)
        below_plane = neighbour_plane(slab - 1, slab * CZ - 1)
        top_plane = masked[:, CZ - 1].reshape(KMAX, -1)
        bottom = masked[:, 0].reshape(KMAX, -1)
        lower_part = -contract(bottom, below_plane)
        middle = contract(masked.reshape(KMAX, -1), images.reshape(KMAX, -1))
        upper_part = -contract(top_plane, above_plane)
        coarse = jnp.concatenate([lower_part, middle, upper_part], axis=1)
        columns = lax.iota(jnp.int32, 3 * KMAX)
        pad_mask = (columns[None, :] == slot_ids[:, None] + KMAX) & jnp.logical_not(live_slots)[:, None]
        return coarse + jnp.where(pad_mask, 1.0, 0.0).astype(jnp.float32)
    coarse = lax.map(slab_rows, jnp.arange(SUBS, dtype=jnp.int32))
    middle = coarse[:, :, KMAX:2 * KMAX]
    blocks = jnp.stack([middle[:, g * BLK:(g + 1) * BLK, g * BLK:(g + 1) * BLK] for g in range(N_GRP)], axis=1)
    factors = jnp.linalg.cholesky(blocks)

    def solve_one(factor, values):
        return jax.scipy.linalg.cho_solve((factor, True), values)
    solve_all = jax.vmap(jax.vmap(solve_one))
    live_rows = slot_ids[None, :] < counts[:, None]
    rhs = right_sides.reshape(SUBS, KMAX, NRHS)
    rhs = jnp.where(live_rows[:, :, None], rhs, 0.0)
    current = damping * solve_all(factors, rhs.reshape(SUBS, N_GRP, BLK, NRHS)).reshape(SUBS, KMAX, NRHS)
    zeros = jnp.zeros((1, KMAX, NRHS), jnp.float32)
    for sweep in range(SWEEPS - 1):
        lower_iter = jnp.concatenate([zeros, current[:-1]], axis=0)
        upper_iter = jnp.concatenate([current[1:], zeros], axis=0)
        stacked = jnp.concatenate([lower_iter, current, upper_iter], axis=1)
        product = jnp.einsum('skc,scr->skr', coarse, stacked, precision=lax.Precision.HIGHEST)
        update = solve_all(factors, (rhs - product).reshape(SUBS, N_GRP, BLK, NRHS)).reshape(SUBS, KMAX, NRHS)
        current = current + damping * update
    return current.reshape(SUBS * KMAX, NRHS)
```

```python
import functools

import jax
import jax.numpy as jnp
import numpy as np
from jax import lax
from jax.experimental import pallas as pl
from jax.experimental.pallas import tpu as pltpu
from jax.sharding import PartitionSpec as P

SWEEPS = 6
damping = 0.7
HIGHEST = lax.Precision.HIGHEST


def remote(src, dst, send_sem, recv_sem, device):
    return pltpu.make_async_remote_copy(
        src_ref=src,
        dst_ref=dst,
        send_sem=send_sem,
        recv_sem=recv_sem,
        device_id=device,
        device_id_type=pl.DeviceIdType.MESH,
    )


def place(subs):
    s, g = lax.axis_index("sub"), lax.axis_index("grp")
    far = g + 2 - 4 * (g // 2)
    near = g + 1 - 2 * lax.rem(g, 2)
    corner = near + 2 - 4 * (near // 2)
    return s, g, far, near, corner, s > 0, s < subs - 1


def greet(s, g, far, near, has_low, has_high):
    barrier = pltpu.get_barrier_semaphore()

    def signal(device):
        pl.semaphore_signal(
            barrier, inc=1, device_id=device, device_id_type=pl.DeviceIdType.MESH
        )

    signal((s, far))
    signal((s, near))

    @pl.when(has_low)
    def _():
        signal((s - 1, g))

    @pl.when(has_high)
    def _():
        signal((s + 1, g))

    peers = 2 + has_low.astype(jnp.int32) + has_high.astype(jnp.int32)
    pl.semaphore_wait(barrier, peers)


def against(left_part, right_part):
    return lax.dot_general(
        left_part, right_part, (((1,), (1,)), ((), ())), preferred_element_type=jnp.float32
    )


def setup_kernel(
    subs, planes, z_ref, shift_ref, spread_ref, pad_ref, e_ref,
    zall, rims, shifts, along, z_send, z_recv, rim_send, rim_recv, sh_send, sh_recv,
):
    s, g, far, near, corner, has_low, has_high = place(subs)
    groups, slots, cells = zall.shape
    width = cells // planes
    own = slots // groups
    chunks = z_recv.shape[1]
    step = slots // chunks

    zall[g] = z_ref[...]
    shifts[g] = shift_ref[...]
    greet(s, g, far, near, has_low, has_high)

    def z_copy(slot, part, kind, to):
        ref = zall.at[slot, pl.ds(part * step, step)]
        return remote(ref, ref, z_send.at[kind, part], z_recv.at[slot, part], (s, to))

    def sh_copy(slot, kind, to):
        ref = shifts.at[slot]
        return remote(ref, ref, sh_send.at[kind], sh_recv.at[slot], (s, to))

    def rim_first(side):
        plane = (planes - 1 if side == 0 else 0) * width
        to = s + 1 if side == 0 else s - 1
        return remote(
            zall.at[g, :, pl.ds(plane, width)], rims.at[side, g],
            rim_send.at[side, 0], rim_recv.at[side, g], (to, g),
        )

    def rim_copy(side, slot, kind, to):
        ref = rims.at[side, slot]
        return remote(ref, ref, rim_send.at[side, kind], rim_recv.at[side, slot], (s, to))

    sends = {0: has_high, 1: has_low}
    holds = {0: has_low, 1: has_high}

    sh_copy(g, 0, far).start()
    sh_copy(g, 1, near).start()
    for part in range(chunks):
        z_copy(g, part, 0, far).start()
    for side in (0, 1):
        @pl.when(sends[side])
        def _(side=side):
            rim_first(side).start()
    for part in range(chunks):
        z_copy(g, part, 1, near).start()

    sh_copy(far, 2, near).wait_recv()
    sh_copy(far, 2, near).start()
    for part in range(chunks):
        z_copy(far, part, 2, near).wait_recv()
        z_copy(far, part, 2, near).start()
    for side in (0, 1):
        @pl.when(holds[side])
        def _(side=side):
            rim_copy(side, g, 1, far).wait_recv()
            rim_copy(side, g, 1, far).start()
            rim_copy(side, g, 2, near).start()

    sh_copy(near, 2, near).wait_recv()
    sh_copy(corner, 2, near).wait_recv()
    for slot in (near, corner):
        for part in range(chunks):
            z_copy(slot, part, 2, near).wait_recv()

    mine = pl.ds(pl.multiple_of(g * own, own), own)
    for y in range(groups):
        along[y] = jnp.dot(zall[y], spread_ref[...], preferred_element_type=jnp.float32)
    total = jnp.zeros((own, slots), jnp.float32)
    for y in range(groups):
        beside = None
        for other in (y - 1, y + 1):
            if 0 <= other < groups:
                beside = along[other] if beside is None else beside + along[other]
        smooth = along[y] if beside is None else along[y] + 0.5 * beside
        centre = (16.0 + shifts[y][0:1, :]) * zall[y].astype(jnp.float32)
        image = (centre - 2.0 * smooth).astype(jnp.bfloat16)
        total = total + against(zall[y, mine, :], image)
    e_ref[:, pl.ds(slots, slots)] = total
    block = pl.ds(pl.multiple_of(slots + g * own, own), own)
    e_ref[:, block] = e_ref[:, block] + pad_ref[...]

    for side in (0, 1):
        @pl.when(holds[side])
        def _(side=side):
            rim_copy(side, far, 3, near).wait_recv()
            rim_copy(side, far, 3, near).start()
    for side in (0, 1):
        columns = pl.ds(2 * side * slots, slots)

        @pl.when(holds[side])
        def _(side=side, columns=columns):
            for slot in (near, corner):
                rim_copy(side, slot, 3, near).wait_recv()
            rows = [
                jnp.dot(
                    rims[side, y], spread_ref[0:width, 0:width],
                    preferred_element_type=jnp.float32,
                )
                for y in range(groups)
            ]
            plane = 0 if side == 0 else (planes - 1) * width
            part = jnp.zeros((own, slots), jnp.float32)
            for y in range(groups):
                beside = [rows[o] for o in (y - 1, y + 1) if 0 <= o < groups]
                smooth = rows[y] + 0.5 * sum(beside[1:], beside[0]) if beside else rows[y]
                part = part + against(
                    zall[y, mine, plane : plane + width], smooth.astype(jnp.bfloat16)
                )
            e_ref[:, columns] = -part

        @pl.when(jnp.logical_not(holds[side]))
        def _(columns=columns):
            e_ref[:, columns] = jnp.zeros((own, slots), jnp.float32)

    for kind in range(3):
        sh_copy(g, kind, far).wait_send()
        for part in range(chunks):
            z_copy(g, part, kind, far).wait_send()
    for side in (0, 1):
        @pl.when(sends[side])
        def _(side=side):
            rim_first(side).wait_send()

        @pl.when(holds[side])
        def _(side=side):
            for kind in (1, 2, 3):
                rim_copy(side, g, kind, far).wait_send()


def sweep_kernel(
    subs, e_ref, inverse_ref, b_ref, x_ref, matrix, held, change, sent, correction,
    send_sem, recv_sem,
):
    s, g, far, near, corner, has_low, has_high = place(subs)
    rows, width = b_ref.shape
    groups = held.shape[1] // 3
    sends = {0: has_high, 1: has_low}
    holds = {0: has_low, 1: has_high}
    start = {0: 0, 1: 2 * groups}
    depth = groups * rows

    def mix(at, kind, ref_slot, to):
        ref = held.at[at, ref_slot]
        return remote(ref, ref, send_sem.at[at, kind], recv_sem.at[at, ref_slot], to)

    def first(at, side):
        to = s + 1 if side == 0 else s - 1
        slot = start[side] + g
        return remote(
            held.at[at, groups + g], held.at[at, slot],
            send_sem.at[at, side], recv_sem.at[at, slot], (to, g),
        )

    greet(s, g, far, near, has_low, has_high)

    full = jnp.dot(inverse_ref[...], e_ref[...], precision=HIGHEST,
                   preferred_element_type=jnp.float32)
    high = full.astype(jnp.bfloat16)
    matrix[0:rows] = high
    matrix[rows : 2 * rows] = (full - high.astype(jnp.float32)).astype(jnp.bfloat16)
    begin = jnp.dot(inverse_ref[...], b_ref[...], precision=HIGHEST,
                    preferred_element_type=jnp.float32)
    correction[...] = begin
    x_ref[...] = damping * begin
    sent[...] = jnp.zeros_like(sent)

    def take(at, begin_slot):
        values = held[at, pl.ds(begin_slot, groups)].reshape(depth, width)
        columns = matrix[:, begin_slot * rows : (begin_slot + groups) * rows]
        both = jnp.dot(columns, values, preferred_element_type=jnp.float32)
        correction[...] = correction[...] - (both[0:rows] + both[rows:])

    def send(at):
        delta = (x_ref[...] - sent[...]).astype(jnp.bfloat16)
        sent[...] = sent[...] + delta.astype(jnp.float32)
        held[at, groups + g] = delta
        for side in (0, 1):
            @pl.when(sends[side])
            def _(side=side):
                first(at, side).start()
        mix(at, 2, groups + g, (s, far)).start()
        mix(at, 3, groups + g, (s, near)).start()

    def collect(at):
        mix(at, 4, groups + far, (s, near)).wait_recv()
        mix(at, 4, groups + far, (s, near)).start()
        for side in (0, 1):
            @pl.when(holds[side])
            def _(side=side):
                slot = start[side] + g
                mix(at, 5 + 3 * side, slot, (s, far)).wait_recv()
                mix(at, 5 + 3 * side, slot, (s, far)).start()
                mix(at, 6 + 3 * side, slot, (s, near)).start()
        for slot in (near, corner):
            mix(at, 4, groups + slot, (s, near)).wait_recv()
        take(at, groups)
        for side in (0, 1):
            @pl.when(holds[side])
            def _(side=side):
                slot = start[side] + far
                mix(at, 7 + 3 * side, slot, (s, near)).wait_recv()
                mix(at, 7 + 3 * side, slot, (s, near)).start()
        for side in (0, 1):
            @pl.when(holds[side])
            def _(side=side):
                for other in (near, corner):
                    mix(at, 7 + 3 * side, start[side] + other, (s, near)).wait_recv()
                take(at, start[side])

    def update():
        x_ref[...] = x_ref[...] + damping * correction[...]

    def sweep(at, carry):
        send(at)
        collect(at)
        update()
        return carry

    send(0)
    send(1)
    collect(0)
    collect(1)
    update()
    lax.fori_loop(2, SWEEPS, sweep, 0)

    def drain(at, carry):
        for kind in (2, 3, 4):
            mix(at, kind, groups + g, (s, far)).wait_send()
        for side in (0, 1):
            @pl.when(sends[side])
            def _(side=side):
                first(at, side).wait_send()

            @pl.when(holds[side])
            def _(side=side):
                for kind in (5, 6, 7):
                    mix(at, kind + 3 * side, groups + g, (s, far)).wait_send()
        return carry

    lax.fori_loop(0, SWEEPS, drain, 0)


def on_device(subs, groups, deflation, shift_field, counts, right_sides):
    slots, planes, _, width = deflation.shape
    rows, sides = right_sides.shape
    cells = planes * width
    live_count = counts[0]
    live_slots = lax.iota(jnp.int32, slots) < live_count
    masked = jnp.where(
        live_slots[:, None], deflation.reshape(slots, cells), jnp.zeros((), deflation.dtype)
    )
    shift = jnp.broadcast_to(shift_field.reshape(1, cells), (8, cells))

    def line(n):
        return np.eye(n) + 0.5 * (np.eye(n, k=1) + np.eye(n, k=-1))

    spread = jnp.asarray(np.kron(line(planes), line(width)), jnp.bfloat16)
    row_slot = lax.axis_index("grp") * rows + lax.iota(jnp.int32, rows)
    dead = row_slot >= live_count
    pad = jnp.where(dead[:, None], jnp.eye(rows, dtype=jnp.float32), 0.0)
    vmem = pl.BlockSpec(memory_space=pltpu.VMEM)
    chunks = 4
    bf16, f32 = jnp.bfloat16, jnp.float32
    matrix = pl.pallas_call(
        functools.partial(setup_kernel, subs, planes),
        out_shape=jax.ShapeDtypeStruct((rows, 3 * slots), f32),
        in_specs=[vmem] * 4,
        out_specs=vmem,
        scratch_shapes=[
            pltpu.VMEM((groups, slots, cells), bf16),
            pltpu.VMEM((2, groups, slots, width), bf16),
            pltpu.VMEM((groups, 8, cells), f32),
            pltpu.VMEM((groups, slots, cells), f32),
            pltpu.SemaphoreType.DMA((3, chunks)),
            pltpu.SemaphoreType.DMA((groups, chunks)),
            pltpu.SemaphoreType.DMA((2, 4)),
            pltpu.SemaphoreType.DMA((2, groups)),
            pltpu.SemaphoreType.DMA((3,)),
            pltpu.SemaphoreType.DMA((groups,)),
        ],
        compiler_params=pltpu.CompilerParams(
            collective_id=0, has_side_effects=True, vmem_limit_bytes=40 * 2**20
        ),
        name="coarse_rows",
    )(masked, shift, spread, pad)

    block = lax.dynamic_slice_in_dim(matrix, slots + lax.axis_index("grp") * rows, rows, 1)
    factor = jnp.linalg.cholesky(block)
    inverse = jax.scipy.linalg.cho_solve((factor, True), jnp.eye(rows, dtype=f32))
    rhs = jnp.where(dead[:, None], 0.0, right_sides)
    count = SWEEPS
    return pl.pallas_call(
        functools.partial(sweep_kernel, subs),
        out_shape=jax.ShapeDtypeStruct((rows, sides), f32),
        in_specs=[vmem] * 3,
        out_specs=vmem,
        scratch_shapes=[
            pltpu.VMEM((2 * rows, 3 * slots), bf16),
            pltpu.VMEM((count, 3 * groups, rows, sides), bf16),
            pltpu.VMEM((8, 128), f32),
            pltpu.VMEM((rows, sides), f32),
            pltpu.VMEM((rows, sides), f32),
            pltpu.SemaphoreType.DMA((count, 11)),
            pltpu.SemaphoreType.DMA((count, 3 * groups)),
        ],
        compiler_params=pltpu.CompilerParams(
            collective_id=1, has_side_effects=True, vmem_limit_bytes=40 * 2**20
        ),
        name="sweeps",
    )(matrix, inverse, rhs)


def solution(mesh):
    in_specs = (
        P(None, "sub", "grp", None),
        P("sub", "grp", None),
        P("sub"),
        P(("sub", "grp"), None),
    )
    out_specs = P(("sub", "grp"), None)
    return jax.shard_map(
        functools.partial(on_device, mesh.shape["sub"], mesh.shape["grp"]),
        mesh=mesh, in_specs=in_specs, out_specs=out_specs, check_vma=False,
    )
```

```python
import functools

import jax
import jax.numpy as jnp
import numpy as np
from jax import lax
from jax.experimental import pallas as pl
from jax.experimental.pallas import tpu as pltpu
from jax.sharding import PartitionSpec as P

SWEEPS = 6
damping = 0.7
HIGHEST = lax.Precision.HIGHEST


def remote(src, dst, send_sem, recv_sem, device):
    return pltpu.make_async_remote_copy(
        src_ref=src,
        dst_ref=dst,
        send_sem=send_sem,
        recv_sem=recv_sem,
        device_id=device,
        device_id_type=pl.DeviceIdType.MESH,
    )


def place(subs):
    s, g = lax.axis_index("sub"), lax.axis_index("grp")
    far = g + 2 - 4 * (g // 2)
    near = g + 1 - 2 * lax.rem(g, 2)
    corner = near + 2 - 4 * (near // 2)
    return s, g, far, near, corner, s > 0, s < subs - 1


def greet(s, g, far, near, has_low, has_high):
    barrier = pltpu.get_barrier_semaphore()

    def signal(device):
        pl.semaphore_signal(
            barrier, inc=1, device_id=device, device_id_type=pl.DeviceIdType.MESH
        )

    signal((s, far))
    signal((s, near))

    @pl.when(has_low)
    def _():
        signal((s - 1, g))

    @pl.when(has_high)
    def _():
        signal((s + 1, g))

    peers = 2 + has_low.astype(jnp.int32) + has_high.astype(jnp.int32)
    pl.semaphore_wait(barrier, peers)


def against(left_part, right_part):
    return lax.dot_general(
        left_part, right_part, (((1,), (1,)), ((), ())), preferred_element_type=jnp.float32
    )


def setup_kernel(
    subs, planes, z_ref, shift_ref, spread_ref, pad_ref, e_ref, inverse_ref,
    zall, rims, shifts, along, z_send, z_recv, rim_send, rim_recv, sh_send, sh_recv,
):
    s, g, far, near, corner, has_low, has_high = place(subs)
    groups, slots, cells = zall.shape
    width = cells // planes
    own = slots // groups
    chunks = z_recv.shape[1]
    step = slots // chunks

    zall[g] = z_ref[...]
    shifts[g] = shift_ref[...]
    greet(s, g, far, near, has_low, has_high)

    def z_copy(slot, part, kind, to):
        ref = zall.at[slot, pl.ds(part * step, step)]
        return remote(ref, ref, z_send.at[kind, part], z_recv.at[slot, part], (s, to))

    def sh_copy(slot, kind, to):
        ref = shifts.at[slot]
        return remote(ref, ref, sh_send.at[kind], sh_recv.at[slot], (s, to))

    def rim_first(side):
        plane = (planes - 1 if side == 0 else 0) * width
        to = s + 1 if side == 0 else s - 1
        return remote(
            zall.at[g, :, pl.ds(plane, width)], rims.at[side, g],
            rim_send.at[side, 0], rim_recv.at[side, g], (to, g),
        )

    def rim_copy(side, slot, kind, to):
        ref = rims.at[side, slot]
        return remote(ref, ref, rim_send.at[side, kind], rim_recv.at[side, slot], (s, to))

    sends = {0: has_high, 1: has_low}
    holds = {0: has_low, 1: has_high}

    sh_copy(g, 0, far).start()
    sh_copy(g, 1, near).start()
    for part in range(chunks):
        z_copy(g, part, 0, far).start()
    for side in (0, 1):
        @pl.when(sends[side])
        def _(side=side):
            rim_first(side).start()
    for part in range(chunks):
        z_copy(g, part, 1, near).start()

    sh_copy(far, 2, near).wait_recv()
    sh_copy(far, 2, near).start()
    for part in range(chunks):
        z_copy(far, part, 2, near).wait_recv()
        z_copy(far, part, 2, near).start()
    for side in (0, 1):
        @pl.when(holds[side])
        def _(side=side):
            rim_copy(side, g, 1, far).wait_recv()
            rim_copy(side, g, 1, far).start()
            rim_copy(side, g, 2, near).start()

    sh_copy(near, 2, near).wait_recv()
    sh_copy(corner, 2, near).wait_recv()
    for slot in (near, corner):
        for part in range(chunks):
            z_copy(slot, part, 2, near).wait_recv()

    mine = pl.ds(pl.multiple_of(g * own, own), own)
    for y in range(groups):
        along[y] = jnp.dot(zall[y], spread_ref[...], preferred_element_type=jnp.float32)
    total = jnp.zeros((own, slots), jnp.float32)
    for y in range(groups):
        beside = None
        for other in (y - 1, y + 1):
            if 0 <= other < groups:
                beside = along[other] if beside is None else beside + along[other]
        smooth = along[y] if beside is None else along[y] + 0.5 * beside
        centre = (16.0 + shifts[y][0:1, :]) * zall[y].astype(jnp.float32)
        image = (centre - 2.0 * smooth).astype(jnp.bfloat16)
        total = total + against(zall[y, mine, :], image)
    e_ref[:, pl.ds(slots, slots)] = total
    block = pl.ds(pl.multiple_of(slots + g * own, own), own)
    e_ref[:, block] = e_ref[:, block] + pad_ref[...]

    for side in (0, 1):
        @pl.when(holds[side])
        def _(side=side):
            rim_copy(side, far, 3, near).wait_recv()
            rim_copy(side, far, 3, near).start()
    inverse_of(e_ref[:, block], inverse_ref)
    for side in (0, 1):
        columns = pl.ds(2 * side * slots, slots)

        @pl.when(holds[side])
        def _(side=side, columns=columns):
            for slot in (near, corner):
                rim_copy(side, slot, 3, near).wait_recv()
            rows = [
                jnp.dot(
                    rims[side, y], spread_ref[0:width, 0:width],
                    preferred_element_type=jnp.float32,
                )
                for y in range(groups)
            ]
            plane = 0 if side == 0 else (planes - 1) * width
            part = jnp.zeros((own, slots), jnp.float32)
            for y in range(groups):
                beside = [rows[o] for o in (y - 1, y + 1) if 0 <= o < groups]
                smooth = rows[y] + 0.5 * sum(beside[1:], beside[0]) if beside else rows[y]
                part = part + against(
                    zall[y, mine, plane : plane + width], smooth.astype(jnp.bfloat16)
                )
            e_ref[:, columns] = -part

        @pl.when(jnp.logical_not(holds[side]))
        def _(columns=columns):
            e_ref[:, columns] = jnp.zeros((own, slots), jnp.float32)

    for kind in range(3):
        sh_copy(g, kind, far).wait_send()
        for part in range(chunks):
            z_copy(g, part, kind, far).wait_send()
    for side in (0, 1):
        @pl.when(sends[side])
        def _(side=side):
            rim_first(side).wait_send()

        @pl.when(holds[side])
        def _(side=side):
            for kind in (1, 2, 3):
                rim_copy(side, g, kind, far).wait_send()


def inverse_of(block, work):
    n = block.shape[0]
    size = 8
    work[...] = block
    lane = lax.broadcasted_iota(jnp.int32, (size, n), 1)
    row = lax.broadcasted_iota(jnp.int32, (size, n), 0)
    every_row = lax.broadcasted_iota(jnp.int32, (n, n), 0)
    every_lane = lax.broadcasted_iota(jnp.int32, (n, n), 1)

    def parts(values):
        first = values.astype(jnp.bfloat16).astype(jnp.float32)
        rest = values - first
        second = rest.astype(jnp.bfloat16).astype(jnp.float32)
        return first, second, rest - second

    def panel(index, carry):
        base = pl.multiple_of(index * size, size)
        original = work[pl.ds(base, size), :]
        columns = [
            jnp.broadcast_to(
                jnp.sum(jnp.where(lane == base + j, original, 0.0), axis=1, keepdims=True),
                (size, n),
            )
            for j in range(size)
        ]
        values = original
        for j in range(size):
            factor = columns[j]
            scale = 1.0 / factor[j : j + 1, :]
            here = row == j

            def eliminate(current):
                pivot = current[j : j + 1, :] * scale
                return jnp.where(here, pivot, current - factor * pivot)

            unit = jnp.where(here, 1.0, 0.0)
            values = eliminate(jnp.where(lane == base + j, unit, values))
            for c in range(j + 1, size):
                columns[c] = eliminate(columns[c])
        inside = (lane >= base) & (lane < base + size)
        left = jnp.where(inside, 0.0, jnp.where(lane < base, -original, original))
        l1, l2, l3 = parts(left)
        r1, r2, r3 = parts(values)
        lefts = jnp.concatenate([l1, l1, l2, l2, l1, l3], axis=0).astype(jnp.bfloat16)
        rights = jnp.concatenate([r1, r2, r1, r2, r3, r1], axis=0).astype(jnp.bfloat16)
        product = lax.dot_general(
            lefts, rights, (((0,), (0,)), ((), ())), preferred_element_type=jnp.float32
        )
        kept = jnp.where((every_lane >= base) & (every_lane < base + size), 0.0, work[...])
        work[...] = kept - product
        work[pl.ds(base, size), :] = values
        return carry

    lax.fori_loop(0, n // size, panel, 0)


def sweep_kernel(
    subs, e_ref, inverse_ref, b_ref, x_ref, matrix, held, sent, correction,
    send_sem, recv_sem,
):
    s, g, far, near, corner, has_low, has_high = place(subs)
    rows, width = b_ref.shape
    groups = held.shape[2] // 3
    halves = held.shape[1]
    half = width // halves
    sends = {0: has_high, 1: has_low}
    holds = {0: has_low, 1: has_high}
    start = {0: 0, 1: 2 * groups}
    depth = groups * rows

    def mix(at, h, kind, slot, to):
        ref = held.at[at, h, slot]
        return remote(ref, ref, send_sem.at[at, h, kind], recv_sem.at[at, h, slot], to)

    def first(at, h, side):
        to = s + 1 if side == 0 else s - 1
        slot = start[side] + g
        return remote(
            held.at[at, h, groups + g], held.at[at, h, slot],
            send_sem.at[at, h, side], recv_sem.at[at, h, slot], (to, g),
        )

    def cut(h):
        return slice(h * half, (h + 1) * half)

    def take(at, h, begin_slot):
        values = held[at, h, pl.ds(begin_slot, groups)].reshape(depth, half)
        columns = matrix[:, begin_slot * rows : (begin_slot + groups) * rows]
        both = jnp.dot(columns, values, preferred_element_type=jnp.float32)
        correction[:, cut(h)] = correction[:, cut(h)] - (both[0:rows] + both[rows:])

    def send(at, h):
        known = sent[:, cut(h)]
        delta = (x_ref[:, cut(h)] - known).astype(jnp.bfloat16)
        sent[:, cut(h)] = known + delta.astype(jnp.float32)
        held[at, h, groups + g] = delta
        for side in (0, 1):
            @pl.when(sends[side])
            def _(side=side):
                first(at, h, side).start()
        mix(at, h, 2, groups + g, (s, far)).start()
        mix(at, h, 3, groups + g, (s, near)).start()

    def pass_first(at, h):
        mix(at, h, 4, groups + far, (s, near)).wait_recv()
        mix(at, h, 4, groups + far, (s, near)).start()
        for side in (0, 1):
            @pl.when(holds[side])
            def _(side=side):
                slot = start[side] + g
                mix(at, h, 5 + 3 * side, slot, (s, far)).wait_recv()
                mix(at, h, 5 + 3 * side, slot, (s, far)).start()
                mix(at, h, 6 + 3 * side, slot, (s, near)).start()

    def pass_second(at, h):
        for side in (0, 1):
            @pl.when(holds[side])
            def _(side=side):
                slot = start[side] + far
                mix(at, h, 7 + 3 * side, slot, (s, near)).wait_recv()
                mix(at, h, 7 + 3 * side, slot, (s, near)).start()

    def take_own(at, h):
        for slot in (near, corner):
            mix(at, h, 4, groups + slot, (s, near)).wait_recv()
        take(at, h, groups)

    def take_sides(at, h):
        for side in (0, 1):
            @pl.when(holds[side])
            def _(side=side):
                for other in (near, corner):
                    mix(at, h, 7 + 3 * side, start[side] + other, (s, near)).wait_recv()
                take(at, h, start[side])

    def update(h):
        x_ref[:, cut(h)] = x_ref[:, cut(h)] + damping * correction[:, cut(h)]

    def sweep(at, last):
        both = range(halves)
        for h in both:
            pass_first(at, h)
        for h in both:
            take_own(at, h)
            pass_second(at, h)
        for h in both:
            take_sides(at, h)
            update(h)
            if not last:
                send(at + 1, h)

    greet(s, g, far, near, has_low, has_high)

    begin = jnp.dot(inverse_ref[...], b_ref[...], precision=HIGHEST,
                    preferred_element_type=jnp.float32)
    correction[...] = begin
    x_ref[...] = damping * begin
    sent[...] = jnp.zeros_like(sent)

    starts = [(at, h) for at in (0, 1) for h in range(halves)]
    for at, h in starts:
        send(at, h)
    full = jnp.dot(inverse_ref[...], e_ref[...], precision=HIGHEST,
                   preferred_element_type=jnp.float32)
    high = full.astype(jnp.bfloat16)
    matrix[0:rows] = high
    matrix[rows : 2 * rows] = (full - high.astype(jnp.float32)).astype(jnp.bfloat16)
    for at, h in starts:
        pass_first(at, h)
    for at, h in starts:
        take_own(at, h)
        pass_second(at, h)
    for h in range(halves):
        take_sides(0, h)
        take_sides(1, h)
        update(h)
        send(2, h)

    def inner(at, carry):
        sweep(at, False)
        return carry

    lax.fori_loop(2, SWEEPS - 1, inner, 0)
    sweep(SWEEPS - 1, True)

    def drain(at, carry):
        for h in range(halves):
            for kind in (2, 3, 4):
                mix(at, h, kind, groups + g, (s, far)).wait_send()
            for side in (0, 1):
                @pl.when(sends[side])
                def _(side=side):
                    first(at, h, side).wait_send()

                @pl.when(holds[side])
                def _(side=side):
                    for kind in (5, 6, 7):
                        mix(at, h, kind + 3 * side, groups + g, (s, far)).wait_send()
        return carry

    lax.fori_loop(0, SWEEPS, drain, 0)


def on_device(subs, groups, deflation, shift_field, counts, right_sides):
    slots, planes, _, width = deflation.shape
    rows, sides = right_sides.shape
    cells = planes * width
    live_count = counts[0]
    live_slots = lax.iota(jnp.int32, slots) < live_count
    masked = jnp.where(
        live_slots[:, None], deflation.reshape(slots, cells), jnp.zeros((), deflation.dtype)
    )
    shift = jnp.broadcast_to(shift_field.reshape(1, cells), (8, cells))

    def line(n):
        return np.eye(n) + 0.5 * (np.eye(n, k=1) + np.eye(n, k=-1))

    spread = jnp.asarray(np.kron(line(planes), line(width)), jnp.bfloat16)
    row_slot = lax.axis_index("grp") * rows + lax.iota(jnp.int32, rows)
    dead = row_slot >= live_count
    pad = jnp.where(dead[:, None], jnp.eye(rows, dtype=jnp.float32), 0.0)
    vmem = pl.BlockSpec(memory_space=pltpu.VMEM)
    chunks = 4
    bf16, f32 = jnp.bfloat16, jnp.float32
    matrix, inverse = pl.pallas_call(
        functools.partial(setup_kernel, subs, planes),
        out_shape=(
            jax.ShapeDtypeStruct((rows, 3 * slots), f32),
            jax.ShapeDtypeStruct((rows, rows), f32),
        ),
        in_specs=[vmem] * 4,
        out_specs=(vmem, vmem),
        scratch_shapes=[
            pltpu.VMEM((groups, slots, cells), bf16),
            pltpu.VMEM((2, groups, slots, width), bf16),
            pltpu.VMEM((groups, 8, cells), f32),
            pltpu.VMEM((groups, slots, cells), f32),
            pltpu.SemaphoreType.DMA((3, chunks)),
            pltpu.SemaphoreType.DMA((groups, chunks)),
            pltpu.SemaphoreType.DMA((2, 4)),
            pltpu.SemaphoreType.DMA((2, groups)),
            pltpu.SemaphoreType.DMA((3,)),
            pltpu.SemaphoreType.DMA((groups,)),
        ],
        compiler_params=pltpu.CompilerParams(
            collective_id=0, has_side_effects=True, vmem_limit_bytes=40 * 2**20
        ),
        name="coarse_rows",
    )(masked, shift, spread, pad)

    rhs = jnp.where(dead[:, None], 0.0, right_sides)
    count, halves = SWEEPS, 2
    return pl.pallas_call(
        functools.partial(sweep_kernel, subs),
        out_shape=jax.ShapeDtypeStruct((rows, sides), f32),
        in_specs=[vmem] * 3,
        out_specs=vmem,
        scratch_shapes=[
            pltpu.VMEM((2 * rows, 3 * slots), bf16),
            pltpu.VMEM((count, halves, 3 * groups, rows, sides // halves), bf16),
            pltpu.VMEM((rows, sides), f32),
            pltpu.VMEM((rows, sides), f32),
            pltpu.SemaphoreType.DMA((count, halves, 11)),
            pltpu.SemaphoreType.DMA((count, halves, 3 * groups)),
        ],
        compiler_params=pltpu.CompilerParams(
            collective_id=1, has_side_effects=True, vmem_limit_bytes=40 * 2**20
        ),
        name="sweeps",
    )(matrix, inverse, rhs)


def solution(mesh):
    in_specs = (
        P(None, "sub", "grp", None),
        P("sub", "grp", None),
        P("sub"),
        P(("sub", "grp"), None),
    )
    out_specs = P(("sub", "grp"), None)
    return jax.shard_map(
        functools.partial(on_device, mesh.shape["sub"], mesh.shape["grp"]),
        mesh=mesh, in_specs=in_specs, out_specs=out_specs, check_vma=False,
    )
```

```python
import functools

import jax
import jax.numpy as jnp
import numpy as np
from jax import lax
from jax.experimental import pallas as pl
from jax.experimental.pallas import tpu as pltpu
from jax.sharding import PartitionSpec as P

SWEEPS = 6
damping = 0.7
HIGHEST = lax.Precision.HIGHEST


def remote(src, dst, send_sem, recv_sem, device):
    return pltpu.make_async_remote_copy(
        src_ref=src,
        dst_ref=dst,
        send_sem=send_sem,
        recv_sem=recv_sem,
        device_id=device,
        device_id_type=pl.DeviceIdType.MESH,
    )


def place(subs):
    s, g = lax.axis_index("sub"), lax.axis_index("grp")
    far = g + 2 - 4 * (g // 2)
    near = g + 1 - 2 * lax.rem(g, 2)
    corner = near + 2 - 4 * (near // 2)
    return s, g, far, near, corner, s > 0, s < subs - 1


def greet(s, g, far, near, has_low, has_high):
    barrier = pltpu.get_barrier_semaphore()

    def signal(device):
        pl.semaphore_signal(
            barrier, inc=1, device_id=device, device_id_type=pl.DeviceIdType.MESH
        )

    signal((s, far))
    signal((s, near))

    @pl.when(has_low)
    def _():
        signal((s - 1, g))

    @pl.when(has_high)
    def _():
        signal((s + 1, g))

    peers = 2 + has_low.astype(jnp.int32) + has_high.astype(jnp.int32)
    pl.semaphore_wait(barrier, peers)


def against(left_part, right_part):
    return lax.dot_general(
        left_part, right_part, (((1,), (1,)), ((), ())), preferred_element_type=jnp.float32
    )


def early_part(
    planes, where, z_ref, shift_ref, spread_ref, pad_ref, e_ref, inverse_ref,
    zall, rims, shifts, along, z_send, z_recv, rim_send, rim_recv, sh_send, sh_recv,
):
    s, g, far, near, corner, has_low, has_high = where
    groups, slots, cells = zall.shape
    width = cells // planes
    own = slots // groups
    chunks = z_recv.shape[1]
    step = slots // chunks

    zall[g] = z_ref[...]
    shifts[g] = shift_ref[...]
    greet(s, g, far, near, has_low, has_high)

    def z_copy(slot, part, kind, to):
        ref = zall.at[slot, pl.ds(pl.multiple_of(part * step, step), step)]
        return remote(ref, ref, z_send.at[kind, part], z_recv.at[slot, part], (s, to))

    def sh_copy(slot, kind, to):
        ref = shifts.at[slot]
        return remote(ref, ref, sh_send.at[kind], sh_recv.at[slot], (s, to))

    def rim_first(side):
        plane = (planes - 1 if side == 0 else 0) * width
        to = s + 1 if side == 0 else s - 1
        return remote(
            zall.at[g, :, pl.ds(plane, width)], rims.at[side, g],
            rim_send.at[side, 0], rim_recv.at[side, g], (to, g),
        )

    def rim_copy(side, slot, kind, to):
        ref = rims.at[side, slot]
        return remote(ref, ref, rim_send.at[side, kind], rim_recv.at[side, slot], (s, to))

    sends = {0: has_high, 1: has_low}
    holds = {0: has_low, 1: has_high}

    sh_copy(g, 0, far).start()
    sh_copy(g, 1, near).start()
    for part in (far, corner, g, near):
        z_copy(g, part, 0, far).start()
    for side in (0, 1):
        @pl.when(sends[side])
        def _(side=side):
            rim_first(side).start()
    for part in (near, g, far, corner):
        z_copy(g, part, 1, near).start()

    sh_copy(far, 2, near).wait_recv()
    sh_copy(far, 2, near).start()
    for part in (near, g):
        z_copy(far, part, 2, near).wait_recv()
        z_copy(far, part, 2, near).start()
    sh_copy(near, 2, near).wait_recv()
    sh_copy(corner, 2, near).wait_recv()
    for slot in (near, corner):
        z_copy(slot, g, 2, near).wait_recv()

    def image_of(field, field_shift, lines, y):
        beside = [lines[o] for o in (y - 1, y + 1) if 0 <= o < groups]
        smooth = lines[y] + 0.5 * sum(beside[1:], beside[0]) if beside else lines[y]
        centre = (16.0 + field_shift) * field.astype(jnp.float32)
        return (centre - 2.0 * smooth).astype(jnp.bfloat16)

    mine = pl.ds(pl.multiple_of(g * own, own), own)
    lines = [
        jnp.dot(zall[y, mine, :], spread_ref[...], preferred_element_type=jnp.float32)
        for y in range(groups)
    ]
    diagonal = pad_ref[...]
    for y in range(groups):
        field = zall[y, mine, :]
        diagonal = diagonal + against(field, image_of(field, shifts[y][0:1, :], lines, y))
    inverse_ref[...] = diagonal
    panels = own // 8
    invert(inverse_ref, 0, panels // 3)
    for part in (far, corner):
        z_copy(far, part, 2, near).wait_recv()
        z_copy(far, part, 2, near).start()
    for side in (0, 1):
        @pl.when(holds[side])
        def _(side=side):
            rim_copy(side, g, 1, far).wait_recv()
            rim_copy(side, g, 1, far).start()
            rim_copy(side, g, 2, near).start()
    invert(inverse_ref, panels // 3, panels)
    yield

    for side in (0, 1):
        @pl.when(holds[side])
        def _(side=side):
            rim_copy(side, far, 3, near).wait_recv()
            rim_copy(side, far, 3, near).start()
    for slot in (near, corner):
        for part in (near, far, corner):
            z_copy(slot, part, 2, near).wait_recv()
    for y in range(groups):
        along[y] = jnp.dot(zall[y], spread_ref[...], preferred_element_type=jnp.float32)
    total = jnp.zeros((own, slots), jnp.float32)
    for y in range(groups):
        image = image_of(zall[y], shifts[y][0:1, :], along, y)
        total = total + against(zall[y, mine, :], image)
    e_ref[:, pl.ds(slots, slots)] = total
    block = pl.ds(pl.multiple_of(slots + g * own, own), own)
    e_ref[:, block] = e_ref[:, block] + pad_ref[...]

    for side in (0, 1):
        columns = pl.ds(2 * side * slots, slots)

        @pl.when(holds[side])
        def _(side=side, columns=columns):
            for slot in (near, corner):
                rim_copy(side, slot, 3, near).wait_recv()
            rows = [
                jnp.dot(
                    rims[side, y], spread_ref[0:width, 0:width],
                    preferred_element_type=jnp.float32,
                )
                for y in range(groups)
            ]
            plane = 0 if side == 0 else (planes - 1) * width
            part = jnp.zeros((own, slots), jnp.float32)
            for y in range(groups):
                beside = [rows[o] for o in (y - 1, y + 1) if 0 <= o < groups]
                smooth = rows[y] + 0.5 * sum(beside[1:], beside[0]) if beside else rows[y]
                part = part + against(
                    zall[y, mine, plane : plane + width], smooth.astype(jnp.bfloat16)
                )
            e_ref[:, columns] = -part

        @pl.when(jnp.logical_not(holds[side]))
        def _(columns=columns):
            e_ref[:, columns] = jnp.zeros((own, slots), jnp.float32)

    yield

    for kind in range(3):
        sh_copy(g, kind, far).wait_send()
        for part in range(chunks):
            z_copy(g, part, kind, far).wait_send()
    for side in (0, 1):
        @pl.when(sends[side])
        def _(side=side):
            rim_first(side).wait_send()

        @pl.when(holds[side])
        def _(side=side):
            for kind in (1, 2, 3):
                rim_copy(side, g, kind, far).wait_send()


def invert(work, begin, end):
    n = work.shape[0]
    size = 8
    lane = lax.broadcasted_iota(jnp.int32, (size, n), 1)
    row = lax.broadcasted_iota(jnp.int32, (size, n), 0)
    every_row = lax.broadcasted_iota(jnp.int32, (n, n), 0)
    every_lane = lax.broadcasted_iota(jnp.int32, (n, n), 1)

    def parts(values):
        first = values.astype(jnp.bfloat16).astype(jnp.float32)
        rest = values - first
        second = rest.astype(jnp.bfloat16).astype(jnp.float32)
        return first, second, rest - second

    def panel(index, carry):
        base = pl.multiple_of(index * size, size)
        original = work[pl.ds(base, size), :]
        columns = [
            jnp.broadcast_to(
                jnp.sum(jnp.where(lane == base + j, original, 0.0), axis=1, keepdims=True),
                (size, n),
            )
            for j in range(size)
        ]
        values = original
        for j in range(size):
            factor = columns[j]
            scale = 1.0 / factor[j : j + 1, :]
            here = row == j

            def eliminate(current):
                pivot = current[j : j + 1, :] * scale
                return jnp.where(here, pivot, current - factor * pivot)

            unit = jnp.where(here, 1.0, 0.0)
            values = eliminate(jnp.where(lane == base + j, unit, values))
            for c in range(j + 1, size):
                columns[c] = eliminate(columns[c])
        inside = (lane >= base) & (lane < base + size)
        left = jnp.where(inside, 0.0, jnp.where(lane < base, -original, original))
        l1, l2, l3 = parts(left)
        r1, r2, r3 = parts(values)
        lefts = jnp.concatenate([l1, l1, l2, l2, l1, l3], axis=0).astype(jnp.bfloat16)
        rights = jnp.concatenate([r1, r2, r1, r2, r3, r1], axis=0).astype(jnp.bfloat16)
        product = lax.dot_general(
            lefts, rights, (((0,), (0,)), ((), ())), preferred_element_type=jnp.float32
        )
        kept = jnp.where((every_lane >= base) & (every_lane < base + size), 0.0, work[...])
        work[...] = kept - product
        work[pl.ds(base, size), :] = values
        return carry

    lax.fori_loop(begin, end, panel, 0)


def kernel(
    subs, planes, z_ref, shift_ref, spread_ref, pad_ref, b_ref, x_ref,
    e_ref, inverse_ref, matrix, held, sent, correction, send_sem, recv_sem, *early_scratch,
):
    where = place(subs)
    s, g, far, near, corner, has_low, has_high = where
    rows, width = b_ref.shape
    groups = held.shape[2] // 3
    halves = held.shape[1]
    half = width // halves
    sends = {0: has_high, 1: has_low}
    holds = {0: has_low, 1: has_high}
    start = {0: 0, 1: 2 * groups}
    depth = groups * rows

    def mix(at, h, kind, slot, to):
        ref = held.at[at, h, slot]
        return remote(ref, ref, send_sem.at[at, h, kind], recv_sem.at[at, h, slot], to)

    def first(at, h, side):
        to = s + 1 if side == 0 else s - 1
        slot = start[side] + g
        return remote(
            held.at[at, h, groups + g], held.at[at, h, slot],
            send_sem.at[at, h, side], recv_sem.at[at, h, slot], (to, g),
        )

    def cut(h):
        return slice(h * half, (h + 1) * half)

    def take(at, h, begin_slot):
        values = held[at, h, pl.ds(begin_slot, groups)].reshape(depth, half)
        columns = matrix[:, begin_slot * rows : (begin_slot + groups) * rows]
        both = jnp.dot(columns, values, preferred_element_type=jnp.float32)
        correction[:, cut(h)] = correction[:, cut(h)] - (both[0:rows] + both[rows:])

    def send(at, h):
        known = sent[:, cut(h)]
        delta = (x_ref[:, cut(h)] - known).astype(jnp.bfloat16)
        sent[:, cut(h)] = known + delta.astype(jnp.float32)
        held[at, h, groups + g] = delta
        for side in (0, 1):
            @pl.when(sends[side])
            def _(side=side):
                first(at, h, side).start()
        mix(at, h, 2, groups + g, (s, far)).start()
        mix(at, h, 3, groups + g, (s, near)).start()

    def pass_first(at, h):
        mix(at, h, 4, groups + far, (s, near)).wait_recv()
        mix(at, h, 4, groups + far, (s, near)).start()
        for side in (0, 1):
            @pl.when(holds[side])
            def _(side=side):
                slot = start[side] + g
                mix(at, h, 5 + 3 * side, slot, (s, far)).wait_recv()
                mix(at, h, 5 + 3 * side, slot, (s, far)).start()
                mix(at, h, 6 + 3 * side, slot, (s, near)).start()

    def pass_second(at, h):
        for side in (0, 1):
            @pl.when(holds[side])
            def _(side=side):
                slot = start[side] + far
                mix(at, h, 7 + 3 * side, slot, (s, near)).wait_recv()
                mix(at, h, 7 + 3 * side, slot, (s, near)).start()

    def take_own(at, h):
        for slot in (near, corner):
            mix(at, h, 4, groups + slot, (s, near)).wait_recv()
        take(at, h, groups)

    def take_sides(at, h):
        for side in (0, 1):
            @pl.when(holds[side])
            def _(side=side):
                for other in (near, corner):
                    mix(at, h, 7 + 3 * side, start[side] + other, (s, near)).wait_recv()
                take(at, h, start[side])

    def update(h):
        x_ref[:, cut(h)] = x_ref[:, cut(h)] + damping * correction[:, cut(h)]

    def sweep(at, last):
        both = range(halves)
        for h in both:
            pass_first(at, h)
        for h in both:
            take_own(at, h)
            pass_second(at, h)
        for h in both:
            take_sides(at, h)
            update(h)
            if not last:
                send(at + 1, h)

    early = early_part(
        planes, where, z_ref, shift_ref, spread_ref, pad_ref, e_ref, inverse_ref, *early_scratch
    )
    next(early)

    begin = jnp.dot(inverse_ref[...], b_ref[...], precision=HIGHEST,
                    preferred_element_type=jnp.float32)
    correction[...] = begin
    x_ref[...] = damping * begin
    sent[...] = jnp.zeros_like(sent)

    starts = [(at, h) for at in (0, 1) for h in range(halves)]
    for at, h in starts:
        send(at, h)
    next(early)
    full = jnp.dot(inverse_ref[...], e_ref[...], precision=HIGHEST,
                   preferred_element_type=jnp.float32)
    high = full.astype(jnp.bfloat16)
    matrix[0:rows] = high
    matrix[rows : 2 * rows] = (full - high.astype(jnp.float32)).astype(jnp.bfloat16)
    for at, h in starts:
        pass_first(at, h)
    for at, h in starts:
        take_own(at, h)
        pass_second(at, h)
    for h in range(halves):
        take_sides(0, h)
        take_sides(1, h)
        update(h)
        send(2, h)

    def inner(at, carry):
        sweep(at, False)
        return carry

    lax.fori_loop(2, SWEEPS - 1, inner, 0)
    sweep(SWEEPS - 1, True)

    def drain(at, carry):
        for h in range(halves):
            for kind in (2, 3, 4):
                mix(at, h, kind, groups + g, (s, far)).wait_send()
            for side in (0, 1):
                @pl.when(sends[side])
                def _(side=side):
                    first(at, h, side).wait_send()

                @pl.when(holds[side])
                def _(side=side):
                    for kind in (5, 6, 7):
                        mix(at, h, kind + 3 * side, groups + g, (s, far)).wait_send()
        return carry

    lax.fori_loop(0, SWEEPS, drain, 0)
    for _ in early:
        pass


def on_device(subs, groups, deflation, shift_field, counts, right_sides):
    slots, planes, _, width = deflation.shape
    rows, sides = right_sides.shape
    cells = planes * width
    live_count = counts[0]
    live_slots = lax.iota(jnp.int32, slots) < live_count
    masked = jnp.where(
        live_slots[:, None], deflation.reshape(slots, cells), jnp.zeros((), deflation.dtype)
    )
    shift = jnp.broadcast_to(shift_field.reshape(1, cells), (8, cells))

    def line(n):
        return np.eye(n) + 0.5 * (np.eye(n, k=1) + np.eye(n, k=-1))

    spread = jnp.asarray(np.kron(line(planes), line(width)), jnp.bfloat16)
    row_slot = lax.axis_index("grp") * rows + lax.iota(jnp.int32, rows)
    dead = row_slot >= live_count
    pad = jnp.where(dead[:, None], jnp.eye(rows, dtype=jnp.float32), 0.0)
    vmem = pl.BlockSpec(memory_space=pltpu.VMEM)
    bf16, f32 = jnp.bfloat16, jnp.float32
    rhs = jnp.where(dead[:, None], 0.0, right_sides)
    count, halves = SWEEPS, 2
    return pl.pallas_call(
        functools.partial(kernel, subs, planes),
        out_shape=jax.ShapeDtypeStruct((rows, sides), f32),
        in_specs=[vmem] * 5,
        out_specs=vmem,
        scratch_shapes=[
            pltpu.VMEM((rows, 3 * slots), f32),
            pltpu.VMEM((rows, rows), f32),
            pltpu.VMEM((2 * rows, 3 * slots), bf16),
            pltpu.VMEM((count, halves, 3 * groups, rows, sides // halves), bf16),
            pltpu.VMEM((rows, sides), f32),
            pltpu.VMEM((rows, sides), f32),
            pltpu.SemaphoreType.DMA((count, halves, 11)),
            pltpu.SemaphoreType.DMA((count, halves, 3 * groups)),
            pltpu.VMEM((groups, slots, cells), bf16),
            pltpu.VMEM((2, groups, slots, width), bf16),
            pltpu.VMEM((groups, 8, cells), f32),
            pltpu.VMEM((groups, slots, cells), f32),
            pltpu.SemaphoreType.DMA((3, groups)),
            pltpu.SemaphoreType.DMA((groups, groups)),
            pltpu.SemaphoreType.DMA((2, 4)),
            pltpu.SemaphoreType.DMA((2, groups)),
            pltpu.SemaphoreType.DMA((3,)),
            pltpu.SemaphoreType.DMA((groups,)),
        ],
        compiler_params=pltpu.CompilerParams(
            collective_id=0, has_side_effects=True, vmem_limit_bytes=40 * 2**20
        ),
        name="schwarz",
    )(masked, shift, spread, pad, rhs)


def solution(mesh):
    in_specs = (
        P(None, "sub", "grp", None),
        P("sub", "grp", None),
        P("sub"),
        P(("sub", "grp"), None),
    )
    out_specs = P(("sub", "grp"), None)
    return jax.shard_map(
        functools.partial(on_device, mesh.shape["sub"], mesh.shape["grp"]),
        mesh=mesh, in_specs=in_specs, out_specs=out_specs, check_vma=False,
    )
```

```python
import functools

import jax
import jax.numpy as jnp
import numpy as np
from jax import lax
from jax.experimental import pallas as pl
from jax.experimental.pallas import tpu as pltpu
from jax.sharding import PartitionSpec as P

SWEEPS = 6
damping = 0.7
HIGHEST = lax.Precision.HIGHEST


def remote(src, dst, send_sem, recv_sem, device):
    return pltpu.make_async_remote_copy(
        src_ref=src,
        dst_ref=dst,
        send_sem=send_sem,
        recv_sem=recv_sem,
        device_id=device,
        device_id_type=pl.DeviceIdType.MESH,
    )


def place(subs):
    s, g = lax.axis_index("sub"), lax.axis_index("grp")
    far = g + 2 - 4 * (g // 2)
    near = g + 1 - 2 * lax.rem(g, 2)
    corner = near + 2 - 4 * (near // 2)
    return s, g, far, near, corner, s > 0, s < subs - 1


def greet(s, g, far, near, has_low, has_high):
    barrier = pltpu.get_barrier_semaphore()

    def signal(device):
        pl.semaphore_signal(
            barrier, inc=1, device_id=device, device_id_type=pl.DeviceIdType.MESH
        )

    signal((s, far))
    signal((s, near))

    @pl.when(has_low)
    def _():
        signal((s - 1, g))

    @pl.when(has_high)
    def _():
        signal((s + 1, g))

    peers = 2 + has_low.astype(jnp.int32) + has_high.astype(jnp.int32)
    pl.semaphore_wait(barrier, peers)


def against(left_part, right_part):
    return lax.dot_general(
        left_part, right_part, (((1,), (1,)), ((), ())), preferred_element_type=jnp.float32
    )


def early_part(
    planes, where, z_ref, shift_ref, spread_ref, pad_ref, e_ref, inverse_ref,
    zall, rims, shifts, along, z_send, z_recv, rim_send, rim_recv, sh_send, sh_recv,
):
    s, g, far, near, corner, has_low, has_high = where
    groups, slots, cells = zall.shape
    width = cells // planes
    own = slots // groups
    chunks = z_recv.shape[1]
    step = slots // chunks

    zall[g] = z_ref[...]
    shifts[g] = shift_ref[...]
    greet(s, g, far, near, has_low, has_high)

    def z_copy(slot, part, kind, to):
        ref = zall.at[slot, pl.ds(pl.multiple_of(part * step, step), step)]
        return remote(ref, ref, z_send.at[kind, part], z_recv.at[slot, part], (s, to))

    def sh_copy(slot, kind, to):
        ref = shifts.at[slot]
        return remote(ref, ref, sh_send.at[kind], sh_recv.at[slot], (s, to))

    def rim_first(side):
        plane = (planes - 1 if side == 0 else 0) * width
        to = s + 1 if side == 0 else s - 1
        return remote(
            zall.at[g, :, pl.ds(plane, width)], rims.at[side, g],
            rim_send.at[side, 0], rim_recv.at[side, g], (to, g),
        )

    def rim_copy(side, slot, kind, to):
        ref = rims.at[side, slot]
        return remote(ref, ref, rim_send.at[side, kind], rim_recv.at[side, slot], (s, to))

    sends = {0: has_high, 1: has_low}
    holds = {0: has_low, 1: has_high}

    sh_copy(g, 0, far).start()
    sh_copy(g, 1, near).start()
    for part in (far, corner, g, near):
        z_copy(g, part, 0, far).start()
    for side in (0, 1):
        @pl.when(sends[side])
        def _(side=side):
            rim_first(side).start()
    for part in (near, g, far, corner):
        z_copy(g, part, 1, near).start()

    sh_copy(far, 2, near).wait_recv()
    sh_copy(far, 2, near).start()
    for part in (near, g):
        z_copy(far, part, 2, near).wait_recv()
        z_copy(far, part, 2, near).start()
    sh_copy(near, 2, near).wait_recv()
    sh_copy(corner, 2, near).wait_recv()
    for slot in (near, corner):
        z_copy(slot, g, 2, near).wait_recv()

    def image_of(field, field_shift, lines, y):
        beside = [lines[o] for o in (y - 1, y + 1) if 0 <= o < groups]
        smooth = lines[y] + 0.5 * sum(beside[1:], beside[0]) if beside else lines[y]
        centre = (16.0 + field_shift) * field.astype(jnp.float32)
        return (centre - 2.0 * smooth).astype(jnp.bfloat16)

    mine = pl.ds(pl.multiple_of(g * own, own), own)
    lines = [
        jnp.dot(zall[y, mine, :], spread_ref[...], preferred_element_type=jnp.float32)
        for y in range(groups)
    ]
    diagonal = pad_ref[...]
    for y in range(groups):
        field = zall[y, mine, :]
        diagonal = diagonal + against(field, image_of(field, shifts[y][0:1, :], lines, y))
    inverse_ref[...] = diagonal
    panels = own // 8
    invert(inverse_ref, 0, panels // 3)
    for part in (far, corner):
        z_copy(far, part, 2, near).wait_recv()
        z_copy(far, part, 2, near).start()
    for side in (0, 1):
        @pl.when(holds[side])
        def _(side=side):
            rim_copy(side, g, 1, far).wait_recv()
            rim_copy(side, g, 1, far).start()
            rim_copy(side, g, 2, near).start()
    invert(inverse_ref, panels // 3, panels)
    yield

    for side in (0, 1):
        @pl.when(holds[side])
        def _(side=side):
            rim_copy(side, far, 3, near).wait_recv()
            rim_copy(side, far, 3, near).start()
    for slot in (near, corner):
        for part in (near, far, corner):
            z_copy(slot, part, 2, near).wait_recv()
    for y in range(groups):
        along[y] = jnp.dot(zall[y], spread_ref[...], preferred_element_type=jnp.float32)
    total = jnp.zeros((own, slots), jnp.float32)
    for y in range(groups):
        image = image_of(zall[y], shifts[y][0:1, :], along, y)
        total = total + against(zall[y, mine, :], image)
    e_ref[:, pl.ds(slots, slots)] = total
    block = pl.ds(pl.multiple_of(slots + g * own, own), own)
    e_ref[:, block] = e_ref[:, block] + pad_ref[...]

    for side in (0, 1):
        columns = pl.ds(2 * side * slots, slots)

        @pl.when(holds[side])
        def _(side=side, columns=columns):
            for slot in (near, corner):
                rim_copy(side, slot, 3, near).wait_recv()
            rows = [
                jnp.dot(
                    rims[side, y], spread_ref[0:width, 0:width],
                    preferred_element_type=jnp.float32,
                )
                for y in range(groups)
            ]
            plane = 0 if side == 0 else (planes - 1) * width
            part = jnp.zeros((own, slots), jnp.float32)
            for y in range(groups):
                beside = [rows[o] for o in (y - 1, y + 1) if 0 <= o < groups]
                smooth = rows[y] + 0.5 * sum(beside[1:], beside[0]) if beside else rows[y]
                part = part + against(
                    zall[y, mine, plane : plane + width], smooth.astype(jnp.bfloat16)
                )
            e_ref[:, columns] = -part

        @pl.when(jnp.logical_not(holds[side]))
        def _(columns=columns):
            e_ref[:, columns] = jnp.zeros((own, slots), jnp.float32)

    yield

    for kind in range(3):
        sh_copy(g, kind, far).wait_send()
        for part in range(chunks):
            z_copy(g, part, kind, far).wait_send()
    for side in (0, 1):
        @pl.when(sends[side])
        def _(side=side):
            rim_first(side).wait_send()

        @pl.when(holds[side])
        def _(side=side):
            for kind in (1, 2, 3):
                rim_copy(side, g, kind, far).wait_send()


def invert(work, begin, end):
    n = work.shape[0]
    size = 8
    lane = lax.broadcasted_iota(jnp.int32, (size, n), 1)
    row = lax.broadcasted_iota(jnp.int32, (size, n), 0)
    every_row = lax.broadcasted_iota(jnp.int32, (n, n), 0)
    every_lane = lax.broadcasted_iota(jnp.int32, (n, n), 1)

    def parts(values):
        first = values.astype(jnp.bfloat16).astype(jnp.float32)
        rest = values - first
        second = rest.astype(jnp.bfloat16).astype(jnp.float32)
        return first, second, rest - second

    def panel(index, carry):
        base = pl.multiple_of(index * size, size)
        original = work[pl.ds(base, size), :]
        columns = [
            jnp.broadcast_to(
                jnp.sum(jnp.where(lane == base + j, original, 0.0), axis=1, keepdims=True),
                (size, n),
            )
            for j in range(size)
        ]
        values = original
        for j in range(size):
            factor = columns[j]
            scale = 1.0 / factor[j : j + 1, :]
            here = row == j

            def eliminate(current):
                pivot = current[j : j + 1, :] * scale
                return jnp.where(here, pivot, current - factor * pivot)

            unit = jnp.where(here, 1.0, 0.0)
            values = eliminate(jnp.where(lane == base + j, unit, values))
            for c in range(j + 1, size):
                columns[c] = eliminate(columns[c])
        inside = (lane >= base) & (lane < base + size)
        left = jnp.where(inside, 0.0, jnp.where(lane < base, -original, original))
        l1, l2, l3 = parts(left)
        r1, r2, r3 = parts(values)
        lefts = jnp.concatenate([l1, l1, l2, l2, l1, l3], axis=0).astype(jnp.bfloat16)
        rights = jnp.concatenate([r1, r2, r1, r2, r3, r1], axis=0).astype(jnp.bfloat16)
        product = lax.dot_general(
            lefts, rights, (((0,), (0,)), ((), ())), preferred_element_type=jnp.float32
        )
        kept = jnp.where((every_lane >= base) & (every_lane < base + size), 0.0, work[...])
        work[...] = kept - product
        work[pl.ds(base, size), :] = values
        return carry

    lax.fori_loop(begin, end, panel, 0)


def kernel(
    subs, planes, z_ref, shift_ref, spread_ref, pad_ref, b_ref, x_ref,
    e_ref, inverse_ref, matrix, held, sent, correction, send_sem, recv_sem, *early_scratch,
):
    where = place(subs)
    s, g, far, near, corner, has_low, has_high = where
    rows, width = b_ref.shape
    groups = held.shape[2] // 3
    halves = held.shape[1]
    half = width // halves
    sends = {0: has_high, 1: has_low}
    holds = {0: has_low, 1: has_high}
    start = {0: 0, 1: 2 * groups}
    depth = groups * rows

    def mix(at, h, kind, slot, to):
        ref = held.at[at, h, slot]
        return remote(ref, ref, send_sem.at[at, h, kind], recv_sem.at[at, h, slot], to)

    def first(at, h, side):
        to = s + 1 if side == 0 else s - 1
        slot = start[side] + g
        return remote(
            held.at[at, h, groups + g], held.at[at, h, slot],
            send_sem.at[at, h, side], recv_sem.at[at, h, slot], (to, g),
        )

    def cut(h):
        return slice(h * half, (h + 1) * half)

    def take(at, h, begin_slot):
        values = held[at, h, pl.ds(begin_slot, groups)].reshape(depth, half)
        columns = matrix[:, begin_slot * rows : (begin_slot + groups) * rows]
        both = jnp.dot(columns, values, preferred_element_type=jnp.float32)
        product = both[0:rows] + both[rows:]
        correction[:, cut(h)] = correction[:, cut(h)] - product
        return product

    def send(at, h, wide=True):
        known = sent[:, cut(h)]
        delta = (x_ref[:, cut(h)] - known).astype(jnp.bfloat16)
        if wide:
            sent[:, cut(h)] = known + delta.astype(jnp.float32)
        held[at, h, groups + g] = delta
        for side in (0, 1) if wide else ():
            @pl.when(sends[side])
            def _(side=side):
                first(at, h, side).start()
        mix(at, h, 2, groups + g, (s, far)).start()
        mix(at, h, 3, groups + g, (s, near)).start()

    def pass_first(at, h, wide=True):
        mix(at, h, 4, groups + far, (s, near)).wait_recv()
        mix(at, h, 4, groups + far, (s, near)).start()
        for side in (0, 1) if wide else ():
            @pl.when(holds[side])
            def _(side=side):
                slot = start[side] + g
                mix(at, h, 5 + 3 * side, slot, (s, far)).wait_recv()
                mix(at, h, 5 + 3 * side, slot, (s, far)).start()
                mix(at, h, 6 + 3 * side, slot, (s, near)).start()

    def pass_second(at, h):
        for side in (0, 1):
            @pl.when(holds[side])
            def _(side=side):
                slot = start[side] + far
                mix(at, h, 7 + 3 * side, slot, (s, near)).wait_recv()
                mix(at, h, 7 + 3 * side, slot, (s, near)).start()

    def take_own(at, h):
        for slot in (near, corner):
            mix(at, h, 4, groups + slot, (s, near)).wait_recv()
        return take(at, h, groups)

    def take_sides(at, h):
        for side in (0, 1):
            @pl.when(holds[side])
            def _(side=side):
                for other in (near, corner):
                    mix(at, h, 7 + 3 * side, start[side] + other, (s, near)).wait_recv()
                take(at, h, start[side])

    def update(h):
        x_ref[:, cut(h)] = x_ref[:, cut(h)] + damping * correction[:, cut(h)]

    def sweep(at, last):
        both = range(halves)
        for h in both:
            pass_first(at, h)
        for h in both:
            take_own(at, h)
            pass_second(at, h)
        for h in both:
            take_sides(at, h)
            update(h)
            if not last:
                send(at + 1, h)

    early = early_part(
        planes, where, z_ref, shift_ref, spread_ref, pad_ref, e_ref, inverse_ref, *early_scratch
    )
    next(early)

    live = 1.0 - jnp.sum(pad_ref[...], axis=0, keepdims=True)
    begin = jnp.dot(inverse_ref[...] * live, b_ref[...], precision=HIGHEST,
                    preferred_element_type=jnp.float32)
    correction[...] = begin
    x_ref[...] = damping * begin
    sent[...] = jnp.zeros_like(sent)

    starts = [(at, h) for at in (0, 1) for h in range(halves)]
    for at, h in starts:
        send(at, h, at == 0)
    next(early)
    full = jnp.dot(inverse_ref[...], e_ref[...], precision=HIGHEST,
                   preferred_element_type=jnp.float32)
    high = full.astype(jnp.bfloat16)
    matrix[0:rows] = high
    matrix[rows : 2 * rows] = (full - high.astype(jnp.float32)).astype(jnp.bfloat16)
    for at, h in starts:
        pass_first(at, h, at == 0)
    rest = []
    for h in range(halves):
        take_own(0, h)
        pass_second(0, h)
    for h in range(halves):
        rest.append(take_own(1, h))
    for h in range(halves):
        take_sides(0, h)
        update(h)
        correction[:, cut(h)] = correction[:, cut(h)] + rest[h]
        send(2, h)

    def inner(at, carry):
        sweep(at, False)
        return carry

    lax.fori_loop(2, SWEEPS - 1, inner, 0)
    sweep(SWEEPS - 1, True)

    def drain(at, wide=True):
        for h in range(halves):
            for kind in (2, 3, 4):
                mix(at, h, kind, groups + g, (s, far)).wait_send()
            for side in (0, 1) if wide else ():
                @pl.when(sends[side])
                def _(side=side):
                    first(at, h, side).wait_send()

                @pl.when(holds[side])
                def _(side=side):
                    for kind in (5, 6, 7):
                        mix(at, h, kind + 3 * side, groups + g, (s, far)).wait_send()

    def drained(at, carry):
        drain(at)
        return carry

    drain(0)
    drain(1, False)
    lax.fori_loop(2, SWEEPS, drained, 0)
    for _ in early:
        pass


def on_device(subs, groups, deflation, shift_field, counts, right_sides):
    slots, planes, _, width = deflation.shape
    rows, sides = right_sides.shape
    cells = planes * width
    live_count = counts[0]
    live_slots = lax.iota(jnp.int32, slots) < live_count
    masked = jnp.where(
        live_slots[:, None], deflation.reshape(slots, cells), jnp.zeros((), deflation.dtype)
    )
    shift = jnp.broadcast_to(shift_field.reshape(1, cells), (8, cells))

    def line(n):
        return np.eye(n) + 0.5 * (np.eye(n, k=1) + np.eye(n, k=-1))

    spread = jnp.asarray(np.kron(line(planes), line(width)), jnp.bfloat16)
    row_slot = lax.axis_index("grp") * rows + lax.iota(jnp.int32, rows)
    dead = row_slot >= live_count
    pad = jnp.where(dead[:, None], jnp.eye(rows, dtype=jnp.float32), 0.0)
    vmem = pl.BlockSpec(memory_space=pltpu.VMEM)
    bf16, f32 = jnp.bfloat16, jnp.float32
    count, halves = SWEEPS, 2
    return pl.pallas_call(
        functools.partial(kernel, subs, planes),
        out_shape=jax.ShapeDtypeStruct((rows, sides), f32),
        in_specs=[vmem] * 5,
        out_specs=vmem,
        scratch_shapes=[
            pltpu.VMEM((rows, 3 * slots), f32),
            pltpu.VMEM((rows, rows), f32),
            pltpu.VMEM((2 * rows, 3 * slots), bf16),
            pltpu.VMEM((count, halves, 3 * groups, rows, sides // halves), bf16),
            pltpu.VMEM((rows, sides), f32),
            pltpu.VMEM((rows, sides), f32),
            pltpu.SemaphoreType.DMA((count, halves, 11)),
            pltpu.SemaphoreType.DMA((count, halves, 3 * groups)),
            pltpu.VMEM((groups, slots, cells), bf16),
            pltpu.VMEM((2, groups, slots, width), bf16),
            pltpu.VMEM((groups, 8, cells), f32),
            pltpu.VMEM((groups, slots, cells), f32),
            pltpu.SemaphoreType.DMA((3, groups)),
            pltpu.SemaphoreType.DMA((groups, groups)),
            pltpu.SemaphoreType.DMA((2, 4)),
            pltpu.SemaphoreType.DMA((2, groups)),
            pltpu.SemaphoreType.DMA((3,)),
            pltpu.SemaphoreType.DMA((groups,)),
        ],
        compiler_params=pltpu.CompilerParams(
            collective_id=0, has_side_effects=True, vmem_limit_bytes=40 * 2**20
        ),
        name="schwarz",
    )(masked, shift, spread, pad, right_sides)


def solution(mesh):
    in_specs = (
        P(None, "sub", "grp", None),
        P("sub", "grp", None),
        P("sub"),
        P(("sub", "grp"), None),
    )
    out_specs = P(("sub", "grp"), None)
    return jax.shard_map(
        functools.partial(on_device, mesh.shape["sub"], mesh.shape["grp"]),
        mesh=mesh, in_specs=in_specs, out_specs=out_specs, check_vma=False,
    )
```

```python
import functools

import jax
import jax.numpy as jnp
import numpy as np
from jax import lax
from jax.experimental import pallas as pl
from jax.experimental.pallas import tpu as pltpu
from jax.sharding import PartitionSpec as P

SWEEPS = 6
damping = 0.7
HIGHEST = lax.Precision.HIGHEST


def remote(src, dst, send_sem, recv_sem, device):
    return pltpu.make_async_remote_copy(
        src_ref=src,
        dst_ref=dst,
        send_sem=send_sem,
        recv_sem=recv_sem,
        device_id=device,
        device_id_type=pl.DeviceIdType.MESH,
    )


def place(subs):
    s, g = lax.axis_index("sub"), lax.axis_index("grp")
    far = g + 2 - 4 * (g // 2)
    near = g + 1 - 2 * lax.rem(g, 2)
    corner = near + 2 - 4 * (near // 2)
    return s, g, far, near, corner, s > 0, s < subs - 1


def greet(s, g, far, near, has_low, has_high):
    barrier = pltpu.get_barrier_semaphore()

    def signal(device):
        pl.semaphore_signal(
            barrier, inc=1, device_id=device, device_id_type=pl.DeviceIdType.MESH
        )

    signal((s, far))
    signal((s, near))

    @pl.when(has_low)
    def _():
        signal((s - 1, g))

    @pl.when(has_high)
    def _():
        signal((s + 1, g))

    peers = 2 + has_low.astype(jnp.int32) + has_high.astype(jnp.int32)
    pl.semaphore_wait(barrier, peers)


def against(left_part, right_part):
    return lax.dot_general(
        left_part, right_part, (((1,), (1,)), ((), ())), preferred_element_type=jnp.float32
    )


def early_part(
    planes, where, z_ref, shift_ref, spread_ref, pad_ref, e_ref, inverse_ref,
    zall, rims, shifts, along, z_send, z_recv, rim_send, rim_recv, sh_send, sh_recv,
):
    s, g, far, near, corner, has_low, has_high = where
    groups, slots, cells = zall.shape
    width = cells // planes
    own = slots // groups
    chunks = z_recv.shape[1]
    step = slots // chunks

    zall[g] = z_ref[...]
    shifts[g] = shift_ref[...]
    greet(s, g, far, near, has_low, has_high)

    def z_copy(slot, part, kind, to):
        ref = zall.at[slot, pl.ds(pl.multiple_of(part * step, step), step)]
        return remote(ref, ref, z_send.at[kind, part], z_recv.at[slot, part], (s, to))

    def sh_copy(slot, kind, to):
        ref = shifts.at[slot]
        return remote(ref, ref, sh_send.at[kind], sh_recv.at[slot], (s, to))

    def rim_first(side):
        plane = (planes - 1 if side == 0 else 0) * width
        to = s + 1 if side == 0 else s - 1
        return remote(
            zall.at[g, :, pl.ds(plane, width)], rims.at[side, g],
            rim_send.at[side, 0], rim_recv.at[side, g], (to, g),
        )

    def rim_copy(side, slot, kind, to):
        ref = rims.at[side, slot]
        return remote(ref, ref, rim_send.at[side, kind], rim_recv.at[side, slot], (s, to))

    sends = {0: has_high, 1: has_low}
    holds = {0: has_low, 1: has_high}

    sh_copy(g, 0, far).start()
    sh_copy(g, 1, near).start()
    for part in (far, corner, g, near):
        z_copy(g, part, 0, far).start()
    for side in (0, 1):
        @pl.when(sends[side])
        def _(side=side):
            rim_first(side).start()
    for part in (near, g, far, corner):
        z_copy(g, part, 1, near).start()

    sh_copy(far, 2, near).wait_recv()
    sh_copy(far, 2, near).start()
    for part in (near, g):
        z_copy(far, part, 2, near).wait_recv()
        z_copy(far, part, 2, near).start()
    sh_copy(near, 2, near).wait_recv()
    sh_copy(corner, 2, near).wait_recv()
    for slot in (near, corner):
        z_copy(slot, g, 2, near).wait_recv()

    def image_of(field, field_shift, lines, y):
        beside = [lines[o] for o in (y - 1, y + 1) if 0 <= o < groups]
        smooth = lines[y] + 0.5 * sum(beside[1:], beside[0]) if beside else lines[y]
        centre = (16.0 + field_shift) * field.astype(jnp.float32)
        return (centre - 2.0 * smooth).astype(jnp.bfloat16)

    mine = pl.ds(pl.multiple_of(g * own, own), own)
    lines = [
        jnp.dot(zall[y, mine, :], spread_ref[...], preferred_element_type=jnp.float32)
        for y in range(groups)
    ]
    diagonal = pad_ref[...]
    for y in range(groups):
        field = zall[y, mine, :]
        diagonal = diagonal + against(field, image_of(field, shifts[y][0:1, :], lines, y))
    inverse_ref[...] = diagonal
    panels = own // 8
    invert(inverse_ref, 0, panels // 3)
    for part in (far, corner):
        z_copy(far, part, 2, near).wait_recv()
        z_copy(far, part, 2, near).start()
    for side in (0, 1):
        @pl.when(holds[side])
        def _(side=side):
            rim_copy(side, g, 1, far).wait_recv()
            rim_copy(side, g, 1, far).start()
            rim_copy(side, g, 2, near).start()
    invert(inverse_ref, panels // 3, panels)
    yield

    for side in (0, 1):
        @pl.when(holds[side])
        def _(side=side):
            rim_copy(side, far, 3, near).wait_recv()
            rim_copy(side, far, 3, near).start()
    for slot in (near, corner):
        for part in (near, far, corner):
            z_copy(slot, part, 2, near).wait_recv()
    for y in range(groups):
        along[y] = jnp.dot(zall[y], spread_ref[...], preferred_element_type=jnp.float32)
    total = jnp.zeros((own, slots), jnp.float32)
    for y in range(groups):
        image = image_of(zall[y], shifts[y][0:1, :], along, y)
        total = total + against(zall[y, mine, :], image)
    e_ref[:, pl.ds(slots, slots)] = total
    block = pl.ds(pl.multiple_of(slots + g * own, own), own)
    e_ref[:, block] = e_ref[:, block] + pad_ref[...]

    for side in (0, 1):
        columns = pl.ds(2 * side * slots, slots)

        @pl.when(holds[side])
        def _(side=side, columns=columns):
            for slot in (near, corner):
                rim_copy(side, slot, 3, near).wait_recv()
            rows = [
                jnp.dot(
                    rims[side, y], spread_ref[0:width, 0:width],
                    preferred_element_type=jnp.float32,
                )
                for y in range(groups)
            ]
            plane = 0 if side == 0 else (planes - 1) * width
            part = jnp.zeros((own, slots), jnp.float32)
            for y in range(groups):
                beside = [rows[o] for o in (y - 1, y + 1) if 0 <= o < groups]
                smooth = rows[y] + 0.5 * sum(beside[1:], beside[0]) if beside else rows[y]
                part = part + against(
                    zall[y, mine, plane : plane + width], smooth.astype(jnp.bfloat16)
                )
            e_ref[:, columns] = -part

        @pl.when(jnp.logical_not(holds[side]))
        def _(columns=columns):
            e_ref[:, columns] = jnp.zeros((own, slots), jnp.float32)

    yield

    for kind in range(3):
        sh_copy(g, kind, far).wait_send()
        for part in range(chunks):
            z_copy(g, part, kind, far).wait_send()
    for side in (0, 1):
        @pl.when(sends[side])
        def _(side=side):
            rim_first(side).wait_send()

        @pl.when(holds[side])
        def _(side=side):
            for kind in (1, 2, 3):
                rim_copy(side, g, kind, far).wait_send()


def invert(work, begin, end):
    n = work.shape[0]
    size = 8
    lane = lax.broadcasted_iota(jnp.int32, (size, n), 1)
    row = lax.broadcasted_iota(jnp.int32, (size, n), 0)
    every_row = lax.broadcasted_iota(jnp.int32, (n, n), 0)
    every_lane = lax.broadcasted_iota(jnp.int32, (n, n), 1)

    def parts(values):
        first = values.astype(jnp.bfloat16).astype(jnp.float32)
        rest = values - first
        second = rest.astype(jnp.bfloat16).astype(jnp.float32)
        return first, second, rest - second

    def panel(index, carry):
        base = pl.multiple_of(index * size, size)
        original = work[pl.ds(base, size), :]
        columns = [
            jnp.broadcast_to(
                jnp.sum(jnp.where(lane == base + j, original, 0.0), axis=1, keepdims=True),
                (size, n),
            )
            for j in range(size)
        ]
        values = original
        for j in range(size):
            factor = columns[j]
            scale = 1.0 / factor[j : j + 1, :]
            here = row == j

            def eliminate(current):
                pivot = current[j : j + 1, :] * scale
                return jnp.where(here, pivot, current - factor * pivot)

            unit = jnp.where(here, 1.0, 0.0)
            values = eliminate(jnp.where(lane == base + j, unit, values))
            for c in range(j + 1, size):
                columns[c] = eliminate(columns[c])
        inside = (lane >= base) & (lane < base + size)
        left = jnp.where(inside, 0.0, jnp.where(lane < base, -original, original))
        l1, l2, l3 = parts(left)
        r1, r2, r3 = parts(values)
        lefts = jnp.concatenate([l1, l1, l2, l2, l1, l3], axis=0).astype(jnp.bfloat16)
        rights = jnp.concatenate([r1, r2, r1, r2, r3, r1], axis=0).astype(jnp.bfloat16)
        product = lax.dot_general(
            lefts, rights, (((0,), (0,)), ((), ())), preferred_element_type=jnp.float32
        )
        kept = jnp.where((every_lane >= base) & (every_lane < base + size), 0.0, work[...])
        work[...] = kept - product
        work[pl.ds(base, size), :] = values
        return carry

    lax.fori_loop(begin, end, panel, 0)


def kernel(
    subs, planes, z_ref, shift_ref, spread_ref, pad_ref, b_ref, x_ref,
    e_ref, inverse_ref, matrix, held, sent, correction, send_sem, recv_sem, *early_scratch,
):
    where = place(subs)
    s, g, far, near, corner, has_low, has_high = where
    rows, width = b_ref.shape
    groups = held.shape[2] // 3
    halves = held.shape[1]
    half = width // halves
    sends = {0: has_high, 1: has_low}
    holds = {0: has_low, 1: has_high}
    start = {0: 0, 1: 2 * groups}
    depth = groups * rows

    def mix(at, h, kind, slot, to):
        ref = held.at[at, h, slot]
        return remote(ref, ref, send_sem.at[at, h, kind], recv_sem.at[at, h, slot], to)

    def first(at, h, side):
        to = s + 1 if side == 0 else s - 1
        slot = start[side] + g
        return remote(
            held.at[at, h, groups + g], held.at[at, h, slot],
            send_sem.at[at, h, side], recv_sem.at[at, h, slot], (to, g),
        )

    def cut(h):
        return slice(h * half, (h + 1) * half)

    def take(at, h, begin_slot):
        values = held[at, h, pl.ds(begin_slot, groups)].reshape(depth, half)
        columns = matrix[:, begin_slot * rows : (begin_slot + groups) * rows]
        both = jnp.dot(columns, values, preferred_element_type=jnp.float32)
        product = both[0:rows] + both[rows:]
        correction[:, cut(h)] = correction[:, cut(h)] - product
        return product

    def send(at, h, wide=True):
        known = sent[:, cut(h)]
        delta = (x_ref[:, cut(h)] - known).astype(jnp.bfloat16)
        if wide:
            sent[:, cut(h)] = known + delta.astype(jnp.float32)
        held[at, h, groups + g] = delta
        for side in (0, 1) if wide else ():
            @pl.when(sends[side])
            def _(side=side):
                first(at, h, side).start()
        mix(at, h, 2, groups + g, (s, far)).start()
        mix(at, h, 3, groups + g, (s, near)).start()

    def pass_first(at, h, wide=True):
        mix(at, h, 4, groups + far, (s, near)).wait_recv()
        mix(at, h, 4, groups + far, (s, near)).start()
        for side in (0, 1) if wide else ():
            @pl.when(holds[side])
            def _(side=side):
                slot = start[side] + g
                mix(at, h, 5 + 3 * side, slot, (s, far)).wait_recv()
                mix(at, h, 5 + 3 * side, slot, (s, far)).start()
                mix(at, h, 6 + 3 * side, slot, (s, near)).start()

    def pass_second(at, h):
        for side in (0, 1):
            @pl.when(holds[side])
            def _(side=side):
                slot = start[side] + far
                mix(at, h, 7 + 3 * side, slot, (s, near)).wait_recv()
                mix(at, h, 7 + 3 * side, slot, (s, near)).start()

    def take_own(at, h):
        for slot in (near, corner):
            mix(at, h, 4, groups + slot, (s, near)).wait_recv()
        return take(at, h, groups)

    def take_sides(at, h):
        for side in (0, 1):
            @pl.when(holds[side])
            def _(side=side):
                for other in (near, corner):
                    mix(at, h, 7 + 3 * side, start[side] + other, (s, near)).wait_recv()
                take(at, h, start[side])

    def update(h):
        x_ref[:, cut(h)] = x_ref[:, cut(h)] + damping * correction[:, cut(h)]

    def sweep(at, last):
        both = range(halves)
        for h in both:
            pass_first(at, h)
        for h in both:
            pass_second(at, h)
            take_own(at, h)
        for h in both:
            take_sides(at, h)
            update(h)
            if not last:
                send(at + 1, h)

    early = early_part(
        planes, where, z_ref, shift_ref, spread_ref, pad_ref, e_ref, inverse_ref, *early_scratch
    )
    next(early)

    live = 1.0 - jnp.sum(pad_ref[...], axis=0, keepdims=True)
    begin = jnp.dot(inverse_ref[...] * live, b_ref[...], precision=HIGHEST,
                    preferred_element_type=jnp.float32)
    correction[...] = begin
    x_ref[...] = damping * begin
    sent[...] = jnp.zeros_like(sent)

    starts = [(at, h) for at in (0, 1) for h in range(halves)]
    for at, h in starts:
        send(at, h, at == 0)
    next(early)
    full = jnp.dot(inverse_ref[...], e_ref[...], precision=HIGHEST,
                   preferred_element_type=jnp.float32)
    high = full.astype(jnp.bfloat16)
    matrix[0:rows] = high
    matrix[rows : 2 * rows] = (full - high.astype(jnp.float32)).astype(jnp.bfloat16)
    for at, h in starts:
        pass_first(at, h, at == 0)
    rest = []
    for h in range(halves):
        take_own(0, h)
        pass_second(0, h)
    for h in range(halves):
        rest.append(take_own(1, h))
    for h in range(halves):
        take_sides(0, h)
        update(h)
        correction[:, cut(h)] = correction[:, cut(h)] + rest[h]
        send(2, h)

    def inner(at, carry):
        sweep(at, False)
        return carry

    lax.fori_loop(2, SWEEPS - 1, inner, 0)
    sweep(SWEEPS - 1, True)

    def drain(at, wide=True):
        for h in range(halves):
            for kind in (2, 3, 4):
                mix(at, h, kind, groups + g, (s, far)).wait_send()
            for side in (0, 1) if wide else ():
                @pl.when(sends[side])
                def _(side=side):
                    first(at, h, side).wait_send()

                @pl.when(holds[side])
                def _(side=side):
                    for kind in (5, 6, 7):
                        mix(at, h, kind + 3 * side, groups + g, (s, far)).wait_send()

    def drained(at, carry):
        drain(at)
        return carry

    drain(0)
    drain(1, False)
    lax.fori_loop(2, SWEEPS, drained, 0)
    for _ in early:
        pass


def on_device(subs, groups, deflation, shift_field, counts, right_sides):
    slots, planes, _, width = deflation.shape
    rows, sides = right_sides.shape
    cells = planes * width
    live_count = counts[0]
    live_slots = lax.iota(jnp.int32, slots) < live_count
    masked = jnp.where(
        live_slots[:, None], deflation.reshape(slots, cells), jnp.zeros((), deflation.dtype)
    )
    shift = jnp.broadcast_to(shift_field.reshape(1, cells), (8, cells))

    def line(n):
        return np.eye(n) + 0.5 * (np.eye(n, k=1) + np.eye(n, k=-1))

    spread = jnp.asarray(np.kron(line(planes), line(width)), jnp.bfloat16)
    row_slot = lax.axis_index("grp") * rows + lax.iota(jnp.int32, rows)
    dead = row_slot >= live_count
    pad = jnp.where(dead[:, None], jnp.eye(rows, dtype=jnp.float32), 0.0)
    vmem = pl.BlockSpec(memory_space=pltpu.VMEM)
    bf16, f32 = jnp.bfloat16, jnp.float32
    count, halves = SWEEPS, 2
    return pl.pallas_call(
        functools.partial(kernel, subs, planes),
        out_shape=jax.ShapeDtypeStruct((rows, sides), f32),
        in_specs=[vmem] * 5,
        out_specs=vmem,
        scratch_shapes=[
            pltpu.VMEM((rows, 3 * slots), f32),
            pltpu.VMEM((rows, rows), f32),
            pltpu.VMEM((2 * rows, 3 * slots), bf16),
            pltpu.VMEM((count, halves, 3 * groups, rows, sides // halves), bf16),
            pltpu.VMEM((rows, sides), f32),
            pltpu.VMEM((rows, sides), f32),
            pltpu.SemaphoreType.DMA((count, halves, 11)),
            pltpu.SemaphoreType.DMA((count, halves, 3 * groups)),
            pltpu.VMEM((groups, slots, cells), bf16),
            pltpu.VMEM((2, groups, slots, width), bf16),
            pltpu.VMEM((groups, 8, cells), f32),
            pltpu.VMEM((groups, slots, cells), f32),
            pltpu.SemaphoreType.DMA((3, groups)),
            pltpu.SemaphoreType.DMA((groups, groups)),
            pltpu.SemaphoreType.DMA((2, 4)),
            pltpu.SemaphoreType.DMA((2, groups)),
            pltpu.SemaphoreType.DMA((3,)),
            pltpu.SemaphoreType.DMA((groups,)),
        ],
        compiler_params=pltpu.CompilerParams(
            collective_id=0, has_side_effects=True, vmem_limit_bytes=40 * 2**20
        ),
        name="schwarz",
    )(masked, shift, spread, pad, right_sides)


def solution(mesh):
    in_specs = (
        P(None, "sub", "grp", None),
        P("sub", "grp", None),
        P("sub"),
        P(("sub", "grp"), None),
    )
    out_specs = P(("sub", "grp"), None)
    return jax.shard_map(
        functools.partial(on_device, mesh.shape["sub"], mesh.shape["grp"]),
        mesh=mesh, in_specs=in_specs, out_specs=out_specs, check_vma=False,
    )
```

```python
import functools

import jax
import jax.numpy as jnp
import numpy as np
from jax import lax
from jax.experimental import pallas as pl
from jax.experimental.pallas import tpu as pltpu
from jax.sharding import PartitionSpec as P

SWEEPS = 6
damping = 0.7
HIGHEST = lax.Precision.HIGHEST


def remote(src, dst, send_sem, recv_sem, device):
    return pltpu.make_async_remote_copy(
        src_ref=src,
        dst_ref=dst,
        send_sem=send_sem,
        recv_sem=recv_sem,
        device_id=device,
        device_id_type=pl.DeviceIdType.MESH,
    )


def place(subs):
    s, g = lax.axis_index("sub"), lax.axis_index("grp")
    far = g + 2 - 4 * (g // 2)
    near = g + 1 - 2 * lax.rem(g, 2)
    corner = near + 2 - 4 * (near // 2)
    return s, g, far, near, corner, s > 0, s < subs - 1


def greet(s, g, far, near, has_low, has_high):
    barrier = pltpu.get_barrier_semaphore()

    def signal(device):
        pl.semaphore_signal(
            barrier, inc=1, device_id=device, device_id_type=pl.DeviceIdType.MESH
        )

    signal((s, far))
    signal((s, near))

    @pl.when(has_low)
    def _():
        signal((s - 1, g))
        signal((s - 1, far))

    @pl.when(has_high)
    def _():
        signal((s + 1, g))
        signal((s + 1, far))

    peers = 2 + 2 * has_low.astype(jnp.int32) + 2 * has_high.astype(jnp.int32)
    pl.semaphore_wait(barrier, peers)


def against(left_part, right_part):
    return lax.dot_general(
        left_part, right_part, (((1,), (1,)), ((), ())), preferred_element_type=jnp.float32
    )


def early_part(
    planes, where, z_ref, shift_ref, spread_ref, pad_ref, e_ref, inverse_ref,
    zall, rims, shifts, along, z_send, z_recv, rim_send, rim_recv, sh_send, sh_recv,
):
    s, g, far, near, corner, has_low, has_high = where
    groups, slots, cells = zall.shape
    width = cells // planes
    own = slots // groups
    chunks = z_recv.shape[1]
    step = slots // chunks

    zall[g] = z_ref[...]
    shifts[g] = shift_ref[...]
    greet(s, g, far, near, has_low, has_high)

    def z_copy(slot, part, kind, to):
        ref = zall.at[slot, pl.ds(pl.multiple_of(part * step, step), step)]
        return remote(ref, ref, z_send.at[kind, part], z_recv.at[slot, part], (s, to))

    def sh_copy(slot, kind, to):
        ref = shifts.at[slot]
        return remote(ref, ref, sh_send.at[kind], sh_recv.at[slot], (s, to))

    def rim_first(side):
        plane = (planes - 1 if side == 0 else 0) * width
        to = s + 1 if side == 0 else s - 1
        return remote(
            zall.at[g, :, pl.ds(plane, width)], rims.at[side, g],
            rim_send.at[side, 0], rim_recv.at[side, g], (to, g),
        )

    def rim_copy(side, slot, kind, to):
        ref = rims.at[side, slot]
        return remote(ref, ref, rim_send.at[side, kind], rim_recv.at[side, slot], (s, to))

    sends = {0: has_high, 1: has_low}
    holds = {0: has_low, 1: has_high}

    sh_copy(g, 0, far).start()
    sh_copy(g, 1, near).start()
    for part in (far, corner, g, near):
        z_copy(g, part, 0, far).start()
    for side in (0, 1):
        @pl.when(sends[side])
        def _(side=side):
            rim_first(side).start()
    for part in (near, g, far, corner):
        z_copy(g, part, 1, near).start()

    sh_copy(far, 2, near).wait_recv()
    sh_copy(far, 2, near).start()
    for part in (near, g):
        z_copy(far, part, 2, near).wait_recv()
        z_copy(far, part, 2, near).start()
    sh_copy(near, 2, near).wait_recv()
    sh_copy(corner, 2, near).wait_recv()
    for slot in (near, corner):
        z_copy(slot, g, 2, near).wait_recv()

    def image_of(field, field_shift, lines, y):
        beside = [lines[o] for o in (y - 1, y + 1) if 0 <= o < groups]
        smooth = lines[y] + 0.5 * sum(beside[1:], beside[0]) if beside else lines[y]
        centre = (16.0 + field_shift) * field.astype(jnp.float32)
        return (centre - 2.0 * smooth).astype(jnp.bfloat16)

    mine = pl.ds(pl.multiple_of(g * own, own), own)
    lines = [
        jnp.dot(zall[y, mine, :], spread_ref[...], preferred_element_type=jnp.float32)
        for y in range(groups)
    ]
    diagonal = pad_ref[...]
    for y in range(groups):
        field = zall[y, mine, :]
        diagonal = diagonal + against(field, image_of(field, shifts[y][0:1, :], lines, y))
    inverse_ref[...] = diagonal
    panels = own // 8
    invert(inverse_ref, 0, panels // 3)
    for part in (far, corner):
        z_copy(far, part, 2, near).wait_recv()
        z_copy(far, part, 2, near).start()
    for side in (0, 1):
        @pl.when(holds[side])
        def _(side=side):
            rim_copy(side, g, 1, far).wait_recv()
            rim_copy(side, g, 1, far).start()
            rim_copy(side, g, 2, near).start()
    invert(inverse_ref, panels // 3, panels)
    yield

    for side in (0, 1):
        @pl.when(holds[side])
        def _(side=side):
            rim_copy(side, far, 3, near).wait_recv()
            rim_copy(side, far, 3, near).start()
    for slot in (near, corner):
        for part in (near, far, corner):
            z_copy(slot, part, 2, near).wait_recv()
    for y in range(groups):
        along[y] = jnp.dot(zall[y], spread_ref[...], preferred_element_type=jnp.float32)
    total = jnp.zeros((own, slots), jnp.float32)
    for y in range(groups):
        image = image_of(zall[y], shifts[y][0:1, :], along, y)
        total = total + against(zall[y, mine, :], image)
    e_ref[:, pl.ds(slots, slots)] = total
    block = pl.ds(pl.multiple_of(slots + g * own, own), own)
    e_ref[:, block] = e_ref[:, block] + pad_ref[...]

    for side in (0, 1):
        columns = pl.ds(2 * side * slots, slots)

        @pl.when(holds[side])
        def _(side=side, columns=columns):
            for slot in (near, corner):
                rim_copy(side, slot, 3, near).wait_recv()
            rows = [
                jnp.dot(
                    rims[side, y], spread_ref[0:width, 0:width],
                    preferred_element_type=jnp.float32,
                )
                for y in range(groups)
            ]
            plane = 0 if side == 0 else (planes - 1) * width
            part = jnp.zeros((own, slots), jnp.float32)
            for y in range(groups):
                beside = [rows[o] for o in (y - 1, y + 1) if 0 <= o < groups]
                smooth = rows[y] + 0.5 * sum(beside[1:], beside[0]) if beside else rows[y]
                part = part + against(
                    zall[y, mine, plane : plane + width], smooth.astype(jnp.bfloat16)
                )
            e_ref[:, columns] = -part

        @pl.when(jnp.logical_not(holds[side]))
        def _(columns=columns):
            e_ref[:, columns] = jnp.zeros((own, slots), jnp.float32)

    yield

    for kind in range(3):
        sh_copy(g, kind, far).wait_send()
        for part in range(chunks):
            z_copy(g, part, kind, far).wait_send()
    for side in (0, 1):
        @pl.when(sends[side])
        def _(side=side):
            rim_first(side).wait_send()

        @pl.when(holds[side])
        def _(side=side):
            for kind in (1, 2, 3):
                rim_copy(side, g, kind, far).wait_send()


def invert(work, begin, end):
    n = work.shape[0]
    size = 8
    lane = lax.broadcasted_iota(jnp.int32, (size, n), 1)
    row = lax.broadcasted_iota(jnp.int32, (size, n), 0)
    every_row = lax.broadcasted_iota(jnp.int32, (n, n), 0)
    every_lane = lax.broadcasted_iota(jnp.int32, (n, n), 1)

    def parts(values):
        first = values.astype(jnp.bfloat16).astype(jnp.float32)
        rest = values - first
        second = rest.astype(jnp.bfloat16).astype(jnp.float32)
        return first, second, rest - second

    def panel(index, carry):
        base = pl.multiple_of(index * size, size)
        original = work[pl.ds(base, size), :]
        columns = [
            jnp.broadcast_to(
                jnp.sum(jnp.where(lane == base + j, original, 0.0), axis=1, keepdims=True),
                (size, n),
            )
            for j in range(size)
        ]
        values = original
        for j in range(size):
            factor = columns[j]
            scale = 1.0 / factor[j : j + 1, :]
            here = row == j

            def eliminate(current):
                pivot = current[j : j + 1, :] * scale
                return jnp.where(here, pivot, current - factor * pivot)

            unit = jnp.where(here, 1.0, 0.0)
            values = eliminate(jnp.where(lane == base + j, unit, values))
            for c in range(j + 1, size):
                columns[c] = eliminate(columns[c])
        inside = (lane >= base) & (lane < base + size)
        left = jnp.where(inside, 0.0, jnp.where(lane < base, -original, original))
        l1, l2, l3 = parts(left)
        r1, r2, r3 = parts(values)
        lefts = jnp.concatenate([l1, l1, l2, l2, l1, l3], axis=0).astype(jnp.bfloat16)
        rights = jnp.concatenate([r1, r2, r1, r2, r3, r1], axis=0).astype(jnp.bfloat16)
        product = lax.dot_general(
            lefts, rights, (((0,), (0,)), ((), ())), preferred_element_type=jnp.float32
        )
        kept = jnp.where((every_lane >= base) & (every_lane < base + size), 0.0, work[...])
        work[...] = kept - product
        work[pl.ds(base, size), :] = values
        return carry

    lax.fori_loop(begin, end, panel, 0)


def kernel(
    subs, planes, z_ref, shift_ref, spread_ref, pad_ref, b_ref, x_ref,
    e_ref, inverse_ref, matrix, held, sent, correction, send_sem, recv_sem, *early_scratch,
):
    where = place(subs)
    s, g, far, near, corner, has_low, has_high = where
    rows, width = b_ref.shape
    groups = held.shape[2] // 3
    halves = held.shape[1]
    half = width // halves
    sends = {0: has_high, 1: has_low}
    holds = {0: has_low, 1: has_high}
    start = {0: 0, 1: 2 * groups}
    depth = groups * rows

    def mix(at, h, kind, slot, to):
        ref = held.at[at, h, slot]
        return remote(ref, ref, send_sem.at[at, h, kind], recv_sem.at[at, h, slot], to)

    def first(at, h, side, kind, to_grp):
        to = s + 1 if side == 0 else s - 1
        slot = start[side] + g
        return remote(
            held.at[at, h, groups + g], held.at[at, h, slot],
            send_sem.at[at, h, kind], recv_sem.at[at, h, slot], (to, to_grp),
        )

    def cut(h):
        return slice(h * half, (h + 1) * half)

    def take(at, h, begin_slot):
        values = held[at, h, pl.ds(begin_slot, groups)].reshape(depth, half)
        columns = matrix[:, begin_slot * rows : (begin_slot + groups) * rows]
        both = jnp.dot(columns, values, preferred_element_type=jnp.float32)
        product = both[0:rows] + both[rows:]
        correction[:, cut(h)] = correction[:, cut(h)] - product
        return product

    def send(at, h, wide=True):
        known = sent[:, cut(h)]
        delta = (x_ref[:, cut(h)] - known).astype(jnp.bfloat16)
        if wide:
            sent[:, cut(h)] = known + delta.astype(jnp.float32)
        held[at, h, groups + g] = delta
        for side in (0, 1) if wide else ():
            @pl.when(sends[side])
            def _(side=side):
                first(at, h, side, side, g).start()
                first(at, h, side, 5 + 3 * side, far).start()
        mix(at, h, 2, groups + g, (s, far)).start()
        mix(at, h, 3, groups + g, (s, near)).start()

    def pass_first(at, h, wide=True):
        mix(at, h, 4, groups + far, (s, near)).wait_recv()
        mix(at, h, 4, groups + far, (s, near)).start()
        for side in (0, 1) if wide else ():
            @pl.when(holds[side])
            def _(side=side):
                slot = start[side] + g
                mix(at, h, 6 + 3 * side, slot, (s, near)).wait_recv()
                mix(at, h, 6 + 3 * side, slot, (s, near)).start()

    def pass_second(at, h):
        for side in (0, 1):
            @pl.when(holds[side])
            def _(side=side):
                slot = start[side] + far
                mix(at, h, 7 + 3 * side, slot, (s, near)).wait_recv()
                mix(at, h, 7 + 3 * side, slot, (s, near)).start()

    def take_own(at, h):
        for slot in (near, corner):
            mix(at, h, 4, groups + slot, (s, near)).wait_recv()
        return take(at, h, groups)

    def take_sides(at, h):
        for side in (0, 1):
            @pl.when(holds[side])
            def _(side=side):
                for other in (near, corner):
                    mix(at, h, 7 + 3 * side, start[side] + other, (s, near)).wait_recv()
                take(at, h, start[side])

    def update(h):
        x_ref[:, cut(h)] = x_ref[:, cut(h)] + damping * correction[:, cut(h)]

    def sweep(at, last):
        both = range(halves)
        for h in both:
            pass_first(at, h)
        for h in both:
            pass_second(at, h)
            take_own(at, h)
        for h in both:
            take_sides(at, h)
            update(h)
            if not last:
                send(at + 1, h)

    early = early_part(
        planes, where, z_ref, shift_ref, spread_ref, pad_ref, e_ref, inverse_ref, *early_scratch
    )
    next(early)

    live = 1.0 - jnp.sum(pad_ref[...], axis=0, keepdims=True)
    begin = jnp.dot(inverse_ref[...] * live, b_ref[...], precision=HIGHEST,
                    preferred_element_type=jnp.float32)
    correction[...] = begin
    x_ref[...] = damping * begin
    sent[...] = jnp.zeros_like(sent)

    starts = [(at, h) for at in (0, 1) for h in range(halves)]
    for at, h in starts:
        send(at, h, at == 0)
    next(early)
    full = jnp.dot(inverse_ref[...], e_ref[...], precision=HIGHEST,
                   preferred_element_type=jnp.float32)
    high = full.astype(jnp.bfloat16)
    matrix[0:rows] = high
    matrix[rows : 2 * rows] = (full - high.astype(jnp.float32)).astype(jnp.bfloat16)
    for at, h in starts:
        pass_first(at, h, at == 0)
    rest = []
    for h in range(halves):
        take_own(0, h)
        pass_second(0, h)
    for h in range(halves):
        rest.append(take_own(1, h))
    for h in range(halves):
        take_sides(0, h)
        update(h)
        correction[:, cut(h)] = correction[:, cut(h)] + rest[h]
        send(2, h)

    def inner(at, carry):
        sweep(at, False)
        return carry

    lax.fori_loop(2, SWEEPS - 1, inner, 0)
    sweep(SWEEPS - 1, True)

    def drain(at, wide=True):
        for h in range(halves):
            for kind in (2, 3, 4):
                mix(at, h, kind, groups + g, (s, far)).wait_send()
            for side in (0, 1) if wide else ():
                @pl.when(sends[side])
                def _(side=side):
                    first(at, h, side, side, g).wait_send()
                    first(at, h, side, 5 + 3 * side, far).wait_send()

                @pl.when(holds[side])
                def _(side=side):
                    for kind in (6, 7):
                        mix(at, h, kind + 3 * side, groups + g, (s, far)).wait_send()

    def drained(at, carry):
        drain(at)
        return carry

    drain(0)
    drain(1, False)
    lax.fori_loop(2, SWEEPS, drained, 0)
    for _ in early:
        pass


def on_device(subs, groups, deflation, shift_field, counts, right_sides):
    slots, planes, _, width = deflation.shape
    rows, sides = right_sides.shape
    cells = planes * width
    live_count = counts[0]
    live_slots = lax.iota(jnp.int32, slots) < live_count
    masked = jnp.where(
        live_slots[:, None], deflation.reshape(slots, cells), jnp.zeros((), deflation.dtype)
    )
    shift = jnp.broadcast_to(shift_field.reshape(1, cells), (8, cells))

    def line(n):
        return np.eye(n) + 0.5 * (np.eye(n, k=1) + np.eye(n, k=-1))

    spread = jnp.asarray(np.kron(line(planes), line(width)), jnp.bfloat16)
    row_slot = lax.axis_index("grp") * rows + lax.iota(jnp.int32, rows)
    dead = row_slot >= live_count
    pad = jnp.where(dead[:, None], jnp.eye(rows, dtype=jnp.float32), 0.0)
    vmem = pl.BlockSpec(memory_space=pltpu.VMEM)
    bf16, f32 = jnp.bfloat16, jnp.float32
    count, halves = SWEEPS, 2
    return pl.pallas_call(
        functools.partial(kernel, subs, planes),
        out_shape=jax.ShapeDtypeStruct((rows, sides), f32),
        in_specs=[vmem] * 5,
        out_specs=vmem,
        scratch_shapes=[
            pltpu.VMEM((rows, 3 * slots), f32),
            pltpu.VMEM((rows, rows), f32),
            pltpu.VMEM((2 * rows, 3 * slots), bf16),
            pltpu.VMEM((count, halves, 3 * groups, rows, sides // halves), bf16),
            pltpu.VMEM((rows, sides), f32),
            pltpu.VMEM((rows, sides), f32),
            pltpu.SemaphoreType.DMA((count, halves, 11)),
            pltpu.SemaphoreType.DMA((count, halves, 3 * groups)),
            pltpu.VMEM((groups, slots, cells), bf16),
            pltpu.VMEM((2, groups, slots, width), bf16),
            pltpu.VMEM((groups, 8, cells), f32),
            pltpu.VMEM((groups, slots, cells), f32),
            pltpu.SemaphoreType.DMA((3, groups)),
            pltpu.SemaphoreType.DMA((groups, groups)),
            pltpu.SemaphoreType.DMA((2, 4)),
            pltpu.SemaphoreType.DMA((2, groups)),
            pltpu.SemaphoreType.DMA((3,)),
            pltpu.SemaphoreType.DMA((groups,)),
        ],
        compiler_params=pltpu.CompilerParams(
            collective_id=0, has_side_effects=True, vmem_limit_bytes=40 * 2**20
        ),
        name="schwarz",
    )(masked, shift, spread, pad, right_sides)


def solution(mesh):
    in_specs = (
        P(None, "sub", "grp", None),
        P("sub", "grp", None),
        P("sub"),
        P(("sub", "grp"), None),
    )
    out_specs = P(("sub", "grp"), None)
    return jax.shard_map(
        functools.partial(on_device, mesh.shape["sub"], mesh.shape["grp"]),
        mesh=mesh, in_specs=in_specs, out_specs=out_specs, check_vma=False,
    )
```
